256 devices in a mesh: seq: 32 (over y, z_hi, core), head: 8 (over x, z_lo).
Axes of the slice: x: 4, y: 4, z: 8 (z_hi: 4, z_lo: 2; z = z_hi * 2 + z_lo), core: 2. Of those that a mesh axis runs over, the one named last changes fastest.
Arguments:
- prompt_q: bfloat16 [512, 5120], P(('seq', 'head')), may hold values from -8 to 8
- prompt_k: bfloat16 [512, 1024], P(('seq', 'head')), may hold values from -8 to 8
- prompt_v: bfloat16 [512, 1024], P(('seq', 'head')), may hold values from -6 to 6
- prompt_grad: bfloat16 [512, 5120], P(('seq', 'head')), may hold values from -6 to 6
- segment_ids: int32 [512], replicated, may hold values from 0 to 127, never falling along the last dimension, each value on 1 to 24 neighbouring positions
- answer_q: bfloat16 [32, 256, 5120], P('seq', None, 'head'), may hold values from -8 to 8
- answer_k: bfloat16 [32, 256, 1024], P('seq', None, 'head'), may hold values from -8 to 8
- answer_v: bfloat16 [32, 256, 1024], P('seq', None, 'head'), may hold values from -6 to 6
- answer_grad: bfloat16 [32, 256, 5120], P('seq', None, 'head'), may hold values from -6 to 6
- answer_lengths: int32 [32], P('seq'), may hold values from 1 to 256, 5120 in all
Outputs:
- prompt_out: bfloat16 [512, 5120], P(('seq', 'head'))
- prompt_dq: bfloat16 [512, 5120], P(('seq', 'head'))
- prompt_dk: bfloat16 [512, 1024], P(('seq', 'head'))
- prompt_dv: bfloat16 [512, 1024], P(('seq', 'head'))
- answer_out: bfloat16 [32, 256, 5120], P('seq', None, 'head')
- answer_dq: bfloat16 [32, 256, 5120], P('seq', None, 'head')
- answer_dk: bfloat16 [32, 256, 1024], P('seq', None, 'head')
- answer_dv: bfloat16 [32, 256, 1024], P('seq', None, 'head')
The draws below stay inside these ranges and needn't reach their ends.
Inputs may be any that keep to these rules, and one draw needn't show every extreme that they name: `segment_ids`: never falls along the prompt; each timestamp segment spans 1 to 24 positions, one exactly 24. `answer_lengths`: one answer has exactly 256 tokens.
All inputs are finite; a program needn't handle non-finite values. No bound on the sum of `answer_lengths` on one device may be relied on, other than what follows from the above.
Results may differ from the reference program's by a relative error of at most 0.038.
Values may be sent and summed in bfloat16 or wider, within the bound.
No kernel may reach another device: no remote copies, remote signals or barrier semaphores. Data moves between devices by JAX's collectives and lax.ppermute only.
A program may use at most 64 MiB of HBM per device.

```python
import math
import jax
import jax.numpy as jnp
import numpy as np
from jax import lax

HEADS = 40
KV_HEADS = 8
HEAD_DIM = 128
ANS_LEN = 256
PROMPT = 512
ANSWERS = 32
SEG_MOST = 24
SEG_COUNT = 128


def draw_prompt_q(key, part):
    key = jax.random.fold_in(key, 1)
    values = 1.5 * jax.random.normal(key, (PROMPT, HEADS * HEAD_DIM), jnp.float32)
    return jnp.clip(values, -8.0, 8.0).astype(jnp.bfloat16)


def draw_answer_q(key, part):
    key = jax.random.fold_in(key, 2)
    values = 1.5 * jax.random.normal(key, (ANSWERS, ANS_LEN, HEADS * HEAD_DIM), jnp.float32)
    return jnp.clip(values, -8.0, 8.0).astype(jnp.bfloat16)


def draw_prompt_k(key, part):
    key = jax.random.fold_in(key, 3)
    values = 1.5 * jax.random.normal(key, (PROMPT, KV_HEADS * HEAD_DIM), jnp.float32)
    return jnp.clip(values, -8.0, 8.0).astype(jnp.bfloat16)


def block_scale(rng, shape, pieces, least, high):
    gain = 1.0
    for dim, parts in pieces:
        heights = jax.random.uniform(jax.random.fold_in(jax.random.fold_in(rng, 6), dim), (parts,), jnp.float32, least / len(pieces), high / len(pieces))
        gain = gain * jnp.repeat(jnp.exp(heights), shape[dim] // parts).reshape((-1,) + (1,) * (len(shape) - 1 - dim))
    return gain


def split_up(count, total, reach, slope):
    portions = [(1 << 20) // math.isqrt(grade ** slope) + 1 for grade in range(2, count + 1)]
    surplus, counts = total - reach - (count - 1), [1] * (count - 1)
    while surplus > 0:
        free = [i for i in range(count - 1) if counts[i] < reach]
        mass, left = sum([portions[i] for i in free]), surplus
        for i in free:
            extra = min(reach - counts[i], max(1, left * portions[i] // mass), surplus)
            counts[i] = counts[i] + extra
            surplus = surplus - extra
    return np.array([reach] + counts)


def ragged_sizes(own_key, amount, total, bound, lean):
    if amount == 2:
        one = jax.random.randint(own_key, (), max(1, total - bound), min(bound, total - 1) + 1)
        return jnp.stack([one, total - one])
    sizes = jnp.asarray(split_up(amount, total, bound, lean), jnp.int32)
    twos = (amount - 1) // 2
    source_of, sink = sizes[1:1 + 2 * twos:2], sizes[2:2 + 2 * twos:2]
    margin = jnp.minimum(source_of - 1, bound - sink)
    shifted = jax.random.randint(jax.random.fold_in(own_key, 1), (twos,), 0, 1 << 20) % (margin + 1)
    sizes = sizes.at[1:1 + 2 * twos:2].set(source_of - shifted).at[2:2 + 2 * twos:2].set(sink + shifted)
    return sizes[jax.random.permutation(jax.random.fold_in(own_key, 2), amount)]


def bell_draw(key, dims, width, most, split=(), kind=jnp.bfloat16):
    gain = block_scale(key, dims, split, -0.22, 0.18) if split else 1.0
    result = jax.random.normal(key, dims, jnp.float32) * width * gain
    return jnp.minimum(jnp.maximum(result, -most), most).astype(kind)


def setup_inputs(seed: int = 0) -> dict:
    splits = jax.random.split(jax.random.key(seed), 11)
    prompt_q = draw_prompt_q(jax.random.fold_in(splits[10], 71), 0)
    prompt_k = draw_prompt_k(jax.random.fold_in(splits[10], 71), 0)
    prompt_v = bell_draw(splits[2], (PROMPT, KV_HEADS * HEAD_DIM), 1.0, 6.0, ((0, 256),))
    prompt_grad = bell_draw(splits[3], (PROMPT, HEADS * HEAD_DIM), 1.0, 6.0, ((0, 256),))
    segment_ids = jnp.searchsorted(jnp.cumsum(ragged_sizes(splits[4], SEG_COUNT, PROMPT, SEG_MOST, 1)), jnp.arange(PROMPT), side="right").astype(jnp.int32)
    answer_q = draw_answer_q(jax.random.fold_in(splits[10], 71), 0)
    answer_k = bell_draw(splits[6], (ANSWERS, ANS_LEN, KV_HEADS * HEAD_DIM), 1.5, 8.0, ((0, 32), (2, 8)))
    answer_v = bell_draw(splits[7], (ANSWERS, ANS_LEN, KV_HEADS * HEAD_DIM), 1.0, 6.0, ((0, 32), (2, 8)))
    answer_grad = bell_draw(splits[8], (ANSWERS, ANS_LEN, HEADS * HEAD_DIM), 1.0, 6.0, ((0, 32), (2, 8)))
    answer_lengths = ragged_sizes(splits[9], ANSWERS, ANSWERS * ANS_LEN * 5 // 8, ANS_LEN, 1).astype(jnp.int32)
    return {"prompt_q": prompt_q, "prompt_k": prompt_k, "prompt_v": prompt_v, "prompt_grad": prompt_grad, "segment_ids": segment_ids, "answer_q": answer_q, "answer_k": answer_k, "answer_v": answer_v, "answer_grad": answer_grad, "answer_lengths": answer_lengths}


def attend(queries, out_grads, key_rows, values, visible, live_rows):
    scaling = 1.0 / math.sqrt(HEAD_DIM)
    query_f = queries.astype(jnp.float32)
    key_f = key_rows.astype(jnp.float32)
    value_f = values.astype(jnp.float32)
    scores = jnp.einsum('rgnd,cgd->gnrc', query_f, key_f) * scaling
    masked = jnp.where(visible[None, None], scores, -jnp.inf)
    top_score = lax.optimization_barrier(jnp.max(masked, axis=-1))
    log_total = top_score + jnp.log(lax.optimization_barrier(jnp.sum(jnp.exp(masked - top_score[..., None]), axis=-1)))
    weights = jnp.exp(masked - log_total[..., None])
    weights_low = lax.optimization_barrier(weights.astype(jnp.bfloat16)).astype(jnp.float32)
    live_f = live_rows[:, None, None, None]
    output = (jnp.einsum('gnrc,cgd->rgnd', weights_low, value_f) * live_f).astype(jnp.bfloat16)
    grads_f = out_grads.astype(jnp.float32) * live_f
    row_delta = jnp.einsum('rgnd,rgnd->gnr', output.astype(jnp.float32), grads_f)
    value_grad = jnp.einsum('gnrc,rgnd->cgd', weights_low, grads_f)
    prob_grad = jnp.einsum('rgnd,cgd->gnrc', grads_f, value_f)
    score_grad = (weights * (prob_grad - row_delta[..., None]) * scaling).astype(jnp.bfloat16)
    score_grad = lax.optimization_barrier(score_grad).astype(jnp.float32)
    query_grad = jnp.einsum('gnrc,cgd->rgnd', score_grad, key_f).astype(jnp.bfloat16)
    key_grad = jnp.einsum('gnrc,rgnd->cgd', score_grad, query_f)
    return (output, query_grad, key_grad, value_grad)

def reference(prompt_q, prompt_k, prompt_v, prompt_grad, segment_ids, answer_q, answer_k, answer_v, answer_grad, answer_lengths):
    group_size = HEADS // KV_HEADS

    def grouped(matrix):
        return matrix.reshape(matrix.shape[0], KV_HEADS, group_size, HEAD_DIM)

    def as_keys(matrix):
        return matrix.reshape(matrix.shape[0], KV_HEADS, HEAD_DIM)
    visible = segment_ids[None, :] <= segment_ids[:, None]
    live_prompt = jnp.ones((PROMPT,), jnp.float32)

    def per_group(packed):
        queries, out_grads, key_rows, values = packed
        return attend(queries, out_grads, key_rows, values, visible, live_prompt)
    query_split = jnp.moveaxis(grouped(prompt_q)[:, :, None], 1, 0)
    grad_split = jnp.moveaxis(grouped(prompt_grad)[:, :, None], 1, 0)
    key_split = jnp.moveaxis(as_keys(prompt_k)[:, :, None], 1, 0)
    value_split = jnp.moveaxis(as_keys(prompt_v)[:, :, None], 1, 0)
    p_out, p_dq, p_dk, p_dv = lax.map(per_group, (query_split, grad_split, key_split, value_split))
    prompt_out = jnp.moveaxis(p_out, 0, 1).reshape(PROMPT, HEADS * HEAD_DIM)
    prompt_dq = jnp.moveaxis(p_dq, 0, 1).reshape(PROMPT, HEADS * HEAD_DIM)
    self_dk = jnp.moveaxis(p_dk, 0, 1).reshape(PROMPT, KV_HEADS, HEAD_DIM)
    self_dv = jnp.moveaxis(p_dv, 0, 1).reshape(PROMPT, KV_HEADS, HEAD_DIM)
    positions = jnp.arange(ANS_LEN, dtype=jnp.int32)
    prompt_visible = jnp.ones((ANS_LEN, PROMPT), jnp.bool_)
    prompt_keys = as_keys(prompt_k)
    prompt_values = as_keys(prompt_v)

    def per_answer(running, packed):
        key_acc, value_acc = running
        queries, out_grads, key_rows, values, length = packed
        live_rows = (positions < length).astype(jnp.float32)
        self_mask = (positions[None, :] <= positions[:, None]) & (positions[None, :] < length)
        visible_all = jnp.concatenate([prompt_visible, self_mask], axis=1)
        all_keys = jnp.concatenate([prompt_keys, as_keys(key_rows)], axis=0)
        all_values = jnp.concatenate([prompt_values, as_keys(values)], axis=0)
        output, query_grad, key_grad, value_grad = attend(grouped(queries), grouped(out_grads), all_keys, all_values, visible_all, live_rows)
        results = (output.reshape(ANS_LEN, HEADS * HEAD_DIM), query_grad.reshape(ANS_LEN, HEADS * HEAD_DIM), key_grad[PROMPT:].astype(jnp.bfloat16).reshape(ANS_LEN, KV_HEADS * HEAD_DIM), value_grad[PROMPT:].astype(jnp.bfloat16).reshape(ANS_LEN, KV_HEADS * HEAD_DIM))
        return ((key_acc + key_grad[:PROMPT], value_acc + value_grad[:PROMPT]), results)
    start_acc = jnp.zeros((PROMPT, KV_HEADS, HEAD_DIM), jnp.float32)
    (key_acc, value_acc), answer_results = lax.scan(per_answer, (start_acc, start_acc), (answer_q, answer_grad, answer_k, answer_v, answer_lengths))
    prompt_dk = (self_dk + key_acc).astype(jnp.bfloat16).reshape(PROMPT, KV_HEADS * HEAD_DIM)
    prompt_dv = (self_dv + value_acc).astype(jnp.bfloat16).reshape(PROMPT, KV_HEADS * HEAD_DIM)
    answer_out, answer_dq, answer_dk, answer_dv = answer_results
    return (prompt_out, prompt_dq, prompt_dk, prompt_dv, answer_out, answer_dq, answer_dk, answer_dv)
```

```python
import math

import jax
import jax.numpy as jnp
from jax import lax
from jax.experimental import pallas as pl
from jax.experimental.pallas import tpu as pltpu
from jax.sharding import Mesh, PartitionSpec as P

HEADS = 40
KV_HEADS = 8
HEAD_DIM = 128
GROUP = HEADS // KV_HEADS
PROMPT = 512
ANS_LEN = 256
HALF = PROMPT // 2
PAIRS = 2 * GROUP
PEERS = 16
NEG = -1e30
SCALING = 1.0 / math.sqrt(HEAD_DIM)
SCALE2 = SCALING / math.log(2.0)
SEQ_AXES = ("y", "zh", "c")
HEAD_AXES = ("x", "zl")
SAME_CORE = ("y", "zh", "x", "zl")
VMEM = pl.BlockSpec(memory_space=pltpu.VMEM)
SMEM = pl.BlockSpec(memory_space=pltpu.SMEM)


def dot(a, b, dims):
    return lax.dot_general(a, b, (dims, ((), ())), preferred_element_type=jnp.float32)


NT = ((1,), (1,))
NN = ((1,), (0,))


def cols(i):
    return slice(i * HEAD_DIM, (i + 1) * HEAD_DIM)


def pack_kernel(q_ref, g_ref, k_ref, v_ref, o_ref):
    q = q_ref[...].astype(jnp.float32)
    g = g_ref[...].astype(jnp.float32)
    zero = jnp.zeros((2, HEAD_DIM), jnp.bfloat16)
    rows = [
        jnp.concatenate([q[r : r + 1], g[r : r + 1]], axis=0).astype(jnp.bfloat16)
        for r in range(2)
    ]
    for h in range(KV_HEADS):
        k = k_ref[:, cols(h)]
        v = v_ref[:, cols(h)]
        for yz in range(PEERS):
            o_ref[yz * KV_HEADS + h, :, cols(0)] = k
            o_ref[yz * KV_HEADS + h, :, cols(1)] = v
            if yz < PAIRS:
                pair = rows[yz // GROUP][:, cols(h * GROUP + yz % GROUP)]
            else:
                pair = zero
            o_ref[yz * KV_HEADS + h, :, cols(2)] = pair


def unpack_kernel(x_ref, out_ref, dq_ref, dk_ref, dv_ref):
    for h in range(KV_HEADS):
        total = jnp.zeros((2, 2 * HEAD_DIM), jnp.float32)
        for yz in range(PEERS):
            total += x_ref[yz * KV_HEADS + h, :, : 2 * HEAD_DIM].astype(jnp.float32)
        dk_ref[:, cols(h)] = total[:, :HEAD_DIM].astype(jnp.bfloat16)
        dv_ref[:, cols(h)] = total[:, HEAD_DIM:].astype(jnp.bfloat16)
        for n in range(GROUP):
            first = x_ref[n * KV_HEADS + h, :, cols(2)].astype(jnp.float32)
            second = x_ref[(GROUP + n) * KV_HEADS + h, :, cols(2)].astype(jnp.float32)
            at = cols(h * GROUP + n)
            out_ref[:, at] = jnp.concatenate([first[:1], second[:1]], axis=0).astype(jnp.bfloat16)
            dq_ref[:, at] = jnp.concatenate([first[1:], second[1:]], axis=0).astype(jnp.bfloat16)


def deinterleave(shape, row_axis):
    i = lax.broadcasted_iota(jnp.int32, shape, row_axis)
    j = lax.broadcasted_iota(jnp.int32, shape, 1 - row_axis)
    source = jnp.where(i < HALF // 2, 2 * i, 2 * i - HALF + 1)
    return (source == j).astype(jnp.bfloat16)


def attend(keys, values, keys_t, values_t, queries, grads, mask):
    scores = mask(dot(keys, queries, NT))
    top = jnp.max(scores, axis=0, keepdims=True)
    weights = jnp.exp2(scores * SCALE2 - top * SCALE2)
    weights = weights * (1.0 / jnp.sum(weights, axis=0, keepdims=True))
    weights_low = weights.astype(jnp.bfloat16)
    out_t = dot(values_t, weights_low, NN)
    product = weights * dot(values, grads, NT)
    delta = jnp.sum(product, axis=0, keepdims=True)
    score_grad = (product - weights * delta).astype(jnp.bfloat16)
    query_grad_t = dot(keys_t, score_grad, NN) * SCALING
    key_grad = dot(score_grad, queries, NN)
    value_grad = dot(weights_low, grads, NN)
    return out_t, query_grad_t, key_grad, value_grad


def main_kernel(
    info_ref, last_ref, own_ref, sib_ref, aq_ref, ak_ref, av_ref, ag_ref,
    aout_ref, adq_ref, adk_ref, adv_ref, down_ref, dsib_ref, pair_ref,
    dk_ref, dv_ref,
):
    length = info_ref[0]
    core = info_ref[1]
    keys = jnp.concatenate([own_ref[:, cols(0)], sib_ref[:, cols(0)], ak_ref[...]], axis=0)
    values = jnp.concatenate([own_ref[:, cols(1)], sib_ref[:, cols(1)], av_ref[...]], axis=0)
    keys_t = keys.T
    values_t = values.T

    moved = dot(deinterleave((HALF, HALF), 0), own_ref[:, cols(2)], NN).astype(jnp.bfloat16)
    j = lax.broadcasted_iota(jnp.int32, (PROMPT, HALF // 2), 0)
    side = jnp.where(j < HALF, core, 1 - core)
    k_pos = ((j & (HALF - 1)) >> 4) * 32 + side * 16 + (j & 15)

    def prompt_mask(scores):
        return jnp.where(k_pos <= last_ref[...], scores, NEG)

    out_t, dq_t, dk, dv = attend(
        keys[:PROMPT], values[:PROMPT], keys_t[:, :PROMPT], values_t[:, :PROMPT],
        moved[: HALF // 2], moved[HALF // 2 :], prompt_mask,
    )
    both = jnp.concatenate([out_t.T, dq_t.T], axis=0).astype(jnp.bfloat16)
    pair_ref[...] = dot(deinterleave((HALF, HALF), 1), both, NN).astype(jnp.bfloat16)
    dk_ref[:PROMPT] = dk
    dv_ref[:PROMPT] = dv
    dk_ref[PROMPT:] = jnp.zeros((ANS_LEN, HEAD_DIM), jnp.float32)
    dv_ref[PROMPT:] = jnp.zeros((ANS_LEN, HEAD_DIM), jnp.float32)

    u = lax.broadcasted_iota(jnp.int32, (ANS_LEN, ANS_LEN), 0)
    t = lax.broadcasted_iota(jnp.int32, (ANS_LEN, ANS_LEN), 1)
    seen = (u <= t) & (u < length)
    live_row = lax.broadcasted_iota(jnp.int32, (ANS_LEN, HEAD_DIM), 0) < length

    def answer_mask(scores):
        return jnp.concatenate(
            [scores[:PROMPT], jnp.where(seen, scores[PROMPT:], NEG)], axis=0
        )

    for n in range(GROUP):
        queries = aq_ref[:, cols(n)]
        grads = ag_ref[:, cols(n)]
        grads = jnp.where(live_row, grads, jnp.zeros_like(grads))
        out_t, dq_t, dk, dv = attend(
            keys, values, keys_t, values_t, queries, grads, answer_mask
        )
        aout_ref[:, cols(n)] = jnp.where(live_row, out_t.T, 0.0).astype(jnp.bfloat16)
        adq_ref[:, cols(n)] = dq_t.T.astype(jnp.bfloat16)
        dk_ref[...] += dk
        dv_ref[...] += dv
    adk_ref[...] = (dk_ref[PROMPT:] * SCALING).astype(jnp.bfloat16)
    adv_ref[...] = dv_ref[PROMPT:].astype(jnp.bfloat16)
    down_ref[:, cols(0)] = dk_ref[:HALF] * SCALING
    down_ref[:, cols(1)] = dv_ref[:HALF]
    dsib_ref[:, cols(0)] = (dk_ref[HALF:PROMPT] * SCALING).astype(jnp.bfloat16)
    dsib_ref[:, cols(1)] = dv_ref[HALF:PROMPT].astype(jnp.bfloat16)


def call(kernel, out_shape, specs, scratch=(), flops=0, moved=0):
    return pl.pallas_call(
        kernel,
        out_shape=out_shape,
        in_specs=specs,
        out_specs=jax.tree.map(lambda _: VMEM, out_shape),
        scratch_shapes=list(scratch),
        cost_estimate=pl.CostEstimate(flops=flops, bytes_accessed=moved, transcendentals=0),
        compiler_params=pltpu.CompilerParams(vmem_limit_bytes=48 * 1024 * 1024),
    )


def bf16(*shape):
    return jax.ShapeDtypeStruct(shape, jnp.bfloat16)


def body(
    prompt_q, prompt_k, prompt_v, prompt_grad, segment_ids,
    answer_q, answer_k, answer_v, answer_grad, answer_lengths,
):
    core = lax.axis_index("c").astype(jnp.int32)
    peer = lax.axis_index(("y", "zh")).astype(jnp.int32)
    wide = HEADS * HEAD_DIM
    narrow = KV_HEADS * HEAD_DIM
    packed = call(pack_kernel, bf16(128, 2, 3 * HEAD_DIM), [VMEM] * 4)(
        prompt_q, prompt_grad, prompt_k, prompt_v
    )
    own = lax.all_to_all(packed, SAME_CORE, split_axis=0, concat_axis=0, tiled=True)
    own = own.reshape(HALF, 3 * HEAD_DIM)
    sibling = lax.ppermute(own, "c", [(0, 1), (1, 0)])

    row = jnp.where(peer >= GROUP, 1, 0)
    segments = lax.dynamic_slice(
        segment_ids.reshape(PEERS, 2, KV_HEADS, 2), (0, core, 0, row), (PEERS, 1, KV_HEADS, 1)
    ).reshape(1, HALF // 2)
    last = jnp.sum(
        (segment_ids[:, None] <= segments).astype(jnp.int32), axis=0, keepdims=True
    ) - 1
    info = jnp.stack([answer_lengths[0], core])

    a_out, a_dq, a_dk, a_dv, d_own, d_sib, pair = call(
        main_kernel,
        (
            bf16(ANS_LEN, GROUP * HEAD_DIM), bf16(ANS_LEN, GROUP * HEAD_DIM),
            bf16(ANS_LEN, HEAD_DIM), bf16(ANS_LEN, HEAD_DIM),
            jax.ShapeDtypeStruct((HALF, 2 * HEAD_DIM), jnp.float32),
            bf16(HALF, 2 * HEAD_DIM), bf16(HALF, HEAD_DIM),
        ),
        [SMEM] + [VMEM] * 7,
        scratch=[
            pltpu.VMEM((PROMPT + ANS_LEN, HEAD_DIM), jnp.float32),
            pltpu.VMEM((PROMPT + ANS_LEN, HEAD_DIM), jnp.float32),
        ],
        flops=1_600_000_000, moved=2_000_000,
    )(info, last, own, sibling, answer_q[0], answer_k[0], answer_v[0], answer_grad[0])

    d_mine = lax.ppermute(d_sib, "c", [(0, 1), (1, 0)])
    terms = (d_own + d_mine.astype(jnp.float32)).astype(jnp.bfloat16)
    back = jnp.concatenate([terms, pair], axis=1).reshape(128, 2, 3 * HEAD_DIM)
    back = lax.all_to_all(back, SAME_CORE, split_axis=0, concat_axis=0, tiled=True)
    p_out, p_dq, p_dk, p_dv = call(
        unpack_kernel, (bf16(2, wide), bf16(2, wide), bf16(2, narrow), bf16(2, narrow)), [VMEM]
    )(back)
    return (p_out, p_dq, p_dk, p_dv, a_out[None], a_dq[None], a_dk[None], a_dv[None])


def solution(mesh):
    grid = Mesh(mesh.devices.reshape(4, 4, 2, 4, 2), SEQ_AXES + HEAD_AXES)
    rows = P(SEQ_AXES + HEAD_AXES, None)
    answers = P(SEQ_AXES, None, HEAD_AXES)
    return jax.shard_map(
        body,
        mesh=grid,
        in_specs=(rows, rows, rows, rows, P(), answers, answers, answers, answers, P(SEQ_AXES)),
        out_specs=(rows, rows, rows, rows, answers, answers, answers, answers),
        check_vma=False,
    )
```

```python
import math

import jax
import jax.numpy as jnp
from jax import lax
from jax.experimental import pallas as pl
from jax.experimental.pallas import tpu as pltpu
from jax.sharding import Mesh, PartitionSpec as P

HEADS = 40
KV_HEADS = 8
HEAD_DIM = 128
GROUP = HEADS // KV_HEADS
PROMPT = 512
ANS_LEN = 256
HALF = PROMPT // 2
PAIRS = 2 * GROUP
PEERS = 16
SENDERS = 128
ROWS = GROUP * ANS_LEN
ALL = ROWS + SENDERS
NEG = -1e30
SCALING = 1.0 / math.sqrt(HEAD_DIM)
SCALE2 = SCALING / math.log(2.0)
SEQ_AXES = ("y", "zh", "c")
HEAD_AXES = ("x", "zl")
SAME_CORE = ("y", "zh", "x", "zl")
OTHER_CORE = [(0, 1), (1, 0)]
VMEM = pl.BlockSpec(memory_space=pltpu.VMEM)
SMEM = pl.BlockSpec(memory_space=pltpu.SMEM)
HBM = pl.BlockSpec(memory_space=pltpu.HBM)
NT = ((1,), (1,))
NN = ((1,), (0,))
BF16 = jnp.bfloat16
F32 = jnp.float32


def dot(a, b, dims):
    return lax.dot_general(a, b, (dims, ((), ())), preferred_element_type=F32)


def cols(i):
    return slice(i * HEAD_DIM, (i + 1) * HEAD_DIM)


def head(n):
    return slice(n * ANS_LEN, min((n + 1) * ANS_LEN, ALL))


def pack_kernel(q_hbm, g_hbm, k_hbm, v_hbm, o_ref, q_ref, g_ref, k_ref, v_ref, sems):
    pairs = ((k_hbm, k_ref), (v_hbm, v_ref), (q_hbm, q_ref), (g_hbm, g_ref))
    copies = [pltpu.make_async_copy(a, b, sems.at[i]) for i, (a, b) in enumerate(pairs)]
    for copy in copies:
        copy.start()
    for copy in copies:
        copy.wait()
    q = q_ref[...].astype(F32)
    g = g_ref[...].astype(F32)
    zero = jnp.zeros((2, HEAD_DIM), BF16)
    rows = [jnp.concatenate([q[r : r + 1], g[r : r + 1]], axis=0).astype(BF16) for r in range(2)]
    for h in range(KV_HEADS):
        k = k_ref[:, cols(h)]
        v = v_ref[:, cols(h)]
        for yz in range(PEERS):
            o_ref[yz * KV_HEADS + h, :, cols(0)] = k
            o_ref[yz * KV_HEADS + h, :, cols(1)] = v
            if yz < PAIRS:
                pair = rows[yz // GROUP][:, cols(h * GROUP + yz % GROUP)]
            else:
                pair = zero
            o_ref[yz * KV_HEADS + h, :, cols(2)] = pair


def unpack_kernel(x_ref, out_ref, dq_ref, dk_ref, dv_ref):
    for h in range(KV_HEADS):
        total = jnp.zeros((2, 2 * HEAD_DIM), F32)
        for yz in range(PEERS):
            total += x_ref[yz * KV_HEADS + h, :, : 2 * HEAD_DIM].astype(F32)
        dk_ref[:, cols(h)] = total[:, :HEAD_DIM].astype(BF16)
        dv_ref[:, cols(h)] = total[:, HEAD_DIM:].astype(BF16)
        for n in range(GROUP):
            first = x_ref[n * KV_HEADS + h, :, cols(2)].astype(F32)
            second = x_ref[(GROUP + n) * KV_HEADS + h, :, cols(2)].astype(F32)
            at = cols(h * GROUP + n)
            out_ref[:, at] = jnp.concatenate([first[:1], second[:1]], axis=0).astype(BF16)
            dq_ref[:, at] = jnp.concatenate([first[1:], second[1:]], axis=0).astype(BF16)


def post_kernel(own_ref, other_ref, pair_ref, o_ref):
    total = (own_ref[...] + other_ref[...].astype(F32)).astype(BF16)
    o_ref[:, :, : 2 * HEAD_DIM] = total.reshape(SENDERS, 2, 2 * HEAD_DIM)
    o_ref[:, :, 2 * HEAD_DIM :] = pair_ref[...].reshape(SENDERS, 2, HEAD_DIM)


def deinterleave(row_axis):
    i = lax.broadcasted_iota(jnp.int32, (HALF, HALF), row_axis)
    j = lax.broadcasted_iota(jnp.int32, (HALF, HALF), 1 - row_axis)
    source = jnp.where(i < SENDERS, 2 * i, 2 * i - HALF + 1)
    return (source == j).astype(BF16)


def seen_by(length):
    u = lax.broadcasted_iota(jnp.int32, (ANS_LEN, ANS_LEN), 0)
    t = lax.broadcasted_iota(jnp.int32, (ANS_LEN, ANS_LEN), 1)
    return (u <= t) & (u < length)


def live_rows(length):
    return lax.broadcasted_iota(jnp.int32, (ANS_LEN, HEAD_DIM), 0) < length


def column_sum(x):
    return jnp.sum(x, axis=0, keepdims=True)


def column_max(x):
    return jnp.max(x, axis=0, keepdims=True)


def own_kernel(
    len_ref, seg_hbm, aq_hbm, ak_hbm, av_hbm, ag_hbm,
    q_ref, g_ref, stat_ref, bias_ref,
    seg_ref, raw_ref, k_ref, v_ref, sems,
):
    pairs = [(seg_hbm, seg_ref), (ak_hbm, k_ref), (av_hbm, v_ref)]
    for n in range(GROUP):
        rows = pl.ds(n * ANS_LEN, ANS_LEN)
        at = pl.ds(n * HEAD_DIM, HEAD_DIM)
        pairs.append((aq_hbm.at[:, at], q_ref.at[rows, :]))
        pairs.append((ag_hbm.at[:, at], raw_ref.at[rows, :]))
    copies = [pltpu.make_async_copy(a, b, sems.at[i]) for i, (a, b) in enumerate(pairs)]
    for copy in copies:
        copy.start()
    length = len_ref[0]
    core = lax.axis_index("c")
    row = jnp.where(lax.axis_index("y") * 4 + lax.axis_index("zh") >= GROUP, 1, 0)

    shape = (PROMPT, PROMPT)
    j = lax.broadcasted_iota(jnp.int32, shape, 0)
    side = jnp.where(j < HALF, core, 1 - core)
    at = ((j & (HALF - 1)) >> 4) * 32 + side * 16 + (j & 15)
    key_pick = (at == lax.broadcasted_iota(jnp.int32, shape, 1)).astype(BF16)
    shape = (SENDERS, PROMPT)
    i = lax.broadcasted_iota(jnp.int32, shape, 0)
    at = (i >> 3) * 32 + core * 16 + (i & 7) * 2 + row
    row_pick = (at == lax.broadcasted_iota(jnp.int32, shape, 1)).astype(BF16)
    copies[0].wait()
    segments = jnp.broadcast_to(seg_ref[...].astype(F32), (SENDERS, PROMPT)).astype(BF16)
    key_segments = dot(key_pick, segments, NT)
    row_segments = dot(segments, row_pick, NT)[:1]
    bias_ref[...] = jnp.where(key_segments <= row_segments, 0.0, NEG)

    seen = seen_by(length)
    live_row = live_rows(length)
    for copy in copies[1:]:
        copy.wait()
    keys = k_ref[...]
    values = v_ref[...]
    for n in range(GROUP):
        grads = raw_ref[head(n)]
        grads = jnp.where(live_row, grads, jnp.zeros_like(grads))
        g_ref[head(n)] = grads
        scores = jnp.where(seen, dot(keys, q_ref[head(n)], NT), NEG)
        top = column_max(scores)
        weights = jnp.exp2(scores * SCALE2 - top * SCALE2)
        stat_ref[n : n + 1] = top
        stat_ref[8 + n : 9 + n] = column_sum(weights)
        stat_ref[16 + n : 17 + n] = column_sum(weights * dot(values, grads, NT))


def near_kernel(
    bias_ref, own_ref, q_ref, g_ref, stat_ref,
    e_ref, far_bias_ref, moved_ref, stat2_ref, q2_ref, g2_ref,
):
    keys = own_ref[:, cols(0)]
    values = own_ref[:, cols(1)]
    moved_ref[...] = dot(deinterleave(0), own_ref[:, cols(2)], NN).astype(BF16)
    far_bias_ref[...] = bias_ref[HALF:]
    q2_ref[...] = q_ref[...]
    g2_ref[...] = g_ref[...]
    for n in range(GROUP + 1):
        if n < GROUP:
            scores = dot(keys, q_ref[head(n)], NT)
            prob_grad = dot(values, g_ref[head(n)], NT)
            old_top = stat_ref[n : n + 1]
            top = jnp.maximum(column_max(scores), old_top)
        else:
            scores = dot(keys, moved_ref[:SENDERS], NT) + bias_ref[:HALF]
            prob_grad = dot(values, moved_ref[SENDERS:], NT)
            top = column_max(scores)
        weights = jnp.exp2(scores * SCALE2 - top * SCALE2)
        total = column_sum(weights)
        moment = column_sum(weights * prob_grad)
        if n < GROUP:
            shift = jnp.exp2((old_top - top) * SCALE2)
            total += stat_ref[8 + n : 9 + n] * shift
            moment += stat_ref[16 + n : 17 + n] * shift
        e_ref[:, head(n)] = weights
        wide = slice(0, weights.shape[1])
        stat2_ref[n : n + 1, wide] = top
        stat2_ref[8 + n : 9 + n, wide] = total
        stat2_ref[16 + n : 17 + n, wide] = moment


def far_kernel(
    bias_ref, own_ref, sib_ref, q_ref, g_ref, e_ref, moved_ref, stat_ref,
    dsib_ref, w_ref, ds_ref, stat2_ref,
):
    keys = sib_ref[:, cols(0)]
    values = sib_ref[:, cols(1)]
    near_values = own_ref[:, cols(1)]
    for n in range(GROUP + 1):
        if n < GROUP:
            scores = dot(keys, q_ref[head(n)], NT)
            grads = g_ref[head(n)]
        else:
            scores = dot(keys, moved_ref[:SENDERS], NT) + bias_ref[...]
            grads = moved_ref[SENDERS:]
        prob_grad = dot(values, grads, NT)
        wide = slice(0, scores.shape[1])
        old_top = stat_ref[n : n + 1, wide]
        top = jnp.maximum(column_max(scores), old_top)
        shift = jnp.exp2((old_top - top) * SCALE2)
        weights = jnp.exp2(scores * SCALE2 - top * SCALE2)
        total = column_sum(weights) + stat_ref[8 + n : 9 + n, wide] * shift
        moment = column_sum(weights * prob_grad) + stat_ref[16 + n : 17 + n, wide] * shift
        inverse = 1.0 / total
        delta = moment * inverse
        if n < GROUP:
            stat2_ref[n : n + 1] = top * SCALE2 + jnp.log2(total)
            stat2_ref[8 + n : 9 + n] = delta
        weights = weights * inverse
        w_ref[HALF:, head(n)] = weights.astype(BF16)
        ds_ref[HALF:, head(n)] = (weights * (prob_grad - delta)).astype(BF16)
        weights = e_ref[:, head(n)] * (shift * inverse)
        w_ref[:HALF, head(n)] = weights.astype(BF16)
        ds_ref[:HALF, head(n)] = (weights * (dot(near_values, grads, NT) - delta)).astype(BF16)
    dk, dv = key_terms(ds_ref[HALF:], w_ref[HALF:], q_ref, g_ref, moved_ref)
    dsib_ref[:, cols(0)] = dk.astype(BF16)
    dsib_ref[:, cols(1)] = dv.astype(BF16)


def key_terms(score_grad, weights, q_ref, g_ref, moved_ref):
    dk = dot(score_grad[:, :ROWS], q_ref[...], NN)
    dk += dot(score_grad[:, ROWS:], moved_ref[:SENDERS], NN)
    dv = dot(weights[:, :ROWS], g_ref[...], NN)
    dv += dot(weights[:, ROWS:], moved_ref[SENDERS:], NN)
    return dk * SCALING, dv


def mine_kernel(
    own_ref, sib_ref, q_ref, g_ref, moved_ref, w_ref, ds_ref, down_ref, pair_ref
):
    dk, dv = key_terms(ds_ref[:HALF], w_ref[:HALF], q_ref, g_ref, moved_ref)
    down_ref[:, cols(0)] = dk
    down_ref[:, cols(1)] = dv
    results = []
    for part, x_ref, factor in ((1, w_ref, 1.0), (0, ds_ref, SCALING)):
        turned = dot(own_ref[:, cols(part)].T, x_ref[:HALF, head(GROUP)], NN)
        turned += dot(sib_ref[:, cols(part)].T, x_ref[HALF:, head(GROUP)], NN)
        results.append((turned * factor).T)
    both = jnp.concatenate(results, axis=0).astype(BF16)
    pair_ref[...] = dot(deinterleave(1), both, NN).astype(BF16)


def rest_kernel(
    len_ref, aq_hbm, ak_hbm, av_hbm, ag_hbm, own_ref, sib_ref, w_ref, ds_ref, stat_ref,
    aout_ref, adq_ref, adk_ref, adv_ref, q_ref, k_ref, v_ref, g_ref, sems,
):
    pairs = ((aq_hbm, q_ref), (ak_hbm, k_ref), (av_hbm, v_ref), (ag_hbm, g_ref))
    copies = [pltpu.make_async_copy(a, b, sems.at[i]) for i, (a, b) in enumerate(pairs)]
    for copy in copies:
        copy.start()
    for copy in copies:
        copy.wait()
    length = len_ref[0]
    seen = seen_by(length)
    live_row = live_rows(length)
    keys = k_ref[...]
    values = v_ref[...]
    keys_t = keys.T
    values_t = values.T
    prompt_keys_t = jnp.concatenate([own_ref[:, cols(0)], sib_ref[:, cols(0)]], axis=0).T
    prompt_values_t = jnp.concatenate([own_ref[:, cols(1)], sib_ref[:, cols(1)]], axis=0).T
    dk = jnp.zeros((ANS_LEN, HEAD_DIM), F32)
    dv = jnp.zeros((ANS_LEN, HEAD_DIM), F32)
    for n in range(GROUP):
        queries = q_ref[:, cols(n)]
        grads = g_ref[:, cols(n)]
        grads = jnp.where(live_row, grads, jnp.zeros_like(grads))
        scores = jnp.where(seen, dot(keys, queries, NT), NEG)
        weights = jnp.exp2(scores * SCALE2 - stat_ref[n : n + 1])
        weights_low = weights.astype(BF16)
        product = dot(values, grads, NT) - stat_ref[8 + n : 9 + n]
        score_grad = (weights * product).astype(BF16)
        out_t = dot(prompt_values_t, w_ref[:, head(n)], NN) + dot(values_t, weights_low, NN)
        dq_t = dot(prompt_keys_t, ds_ref[:, head(n)], NN) + dot(keys_t, score_grad, NN)
        aout_ref[:, cols(n)] = jnp.where(live_row, out_t.T, 0.0).astype(BF16)
        adq_ref[:, cols(n)] = (dq_t * SCALING).T.astype(BF16)
        dk += dot(score_grad, queries, NN)
        dv += dot(weights_low, grads, NN)
    adk_ref[...] = (dk * SCALING).astype(BF16)
    adv_ref[...] = dv.astype(BF16)


def call(kernel, out_shape, specs, scratch=(), flops=0, moved=0, limit=16):
    return pl.pallas_call(
        kernel,
        out_shape=out_shape,
        in_specs=specs,
        out_specs=jax.tree.map(lambda _: VMEM, out_shape),
        scratch_shapes=list(scratch),
        cost_estimate=pl.CostEstimate(flops=flops, bytes_accessed=moved, transcendentals=0),
        compiler_params=pltpu.CompilerParams(vmem_limit_bytes=limit * 1024 * 1024),
    )


def bf16(*shape):
    return jax.ShapeDtypeStruct(shape, BF16)


def vmem(*shape, dtype=BF16):
    return pltpu.VMEM(shape, dtype)


def in_hbm(x):
    return pltpu.with_memory_space_constraint(x, pltpu.HBM)


def in_vmem(x):
    return pltpu.with_memory_space_constraint(x, pltpu.VMEM)


def body(
    prompt_q, prompt_k, prompt_v, prompt_grad, segment_ids,
    answer_q, answer_k, answer_v, answer_grad, answer_lengths,
):
    wide = HEADS * HEAD_DIM
    narrow = KV_HEADS * HEAD_DIM
    group = GROUP * HEAD_DIM
    packed = call(
        pack_kernel,
        bf16(SENDERS, 2, 3 * HEAD_DIM),
        [HBM] * 4,
        scratch=[
            pltpu.VMEM((2, wide), BF16), pltpu.VMEM((2, wide), BF16),
            pltpu.VMEM((2, narrow), BF16), pltpu.VMEM((2, narrow), BF16),
            pltpu.SemaphoreType.DMA((4,)),
        ],
        limit=4,
    )(in_hbm(prompt_q), in_hbm(prompt_grad), in_hbm(prompt_k), in_hbm(prompt_v))
    packed, answer_q = lax.optimization_barrier((packed, answer_q))
    own = lax.all_to_all(packed, SAME_CORE, split_axis=0, concat_axis=0, tiled=True)
    own = own.reshape(HALF, 3 * HEAD_DIM)

    queries, grads, stat, bias = call(
        own_kernel,
        (
            vmem(ROWS, HEAD_DIM), vmem(ROWS, HEAD_DIM), vmem(24, ANS_LEN, dtype=F32),
            vmem(PROMPT, SENDERS, dtype=F32),
        ),
        [SMEM] + [HBM] * 5,
        scratch=[
            pltpu.VMEM((1, PROMPT), jnp.int32), pltpu.VMEM((ROWS, HEAD_DIM), BF16),
            pltpu.VMEM((ANS_LEN, HEAD_DIM), BF16), pltpu.VMEM((ANS_LEN, HEAD_DIM), BF16),
            pltpu.SemaphoreType.DMA((3 + 2 * GROUP,)),
        ],
        flops=400_000_000, moved=2_000_000,
    )(
        answer_lengths, in_hbm(segment_ids.reshape(1, PROMPT)), in_hbm(answer_q[0]),
        in_hbm(answer_k[0]), in_hbm(answer_v[0]), in_hbm(answer_grad[0]),
    )
    own, stat = lax.optimization_barrier((own, stat))
    sibling = lax.ppermute(own, "c", OTHER_CORE)
    exps, bias, moved, stat, queries, grads = call(
        near_kernel,
        (
            vmem(HALF, ALL, dtype=F32), vmem(HALF, SENDERS, dtype=F32), vmem(HALF, HEAD_DIM),
            vmem(24, ANS_LEN, dtype=F32), vmem(ROWS, HEAD_DIM), vmem(ROWS, HEAD_DIM),
        ),
        [VMEM] * 5,
        flops=200_000_000, moved=2_000_000,
    )(bias, own, queries, grads, stat)
    d_sib, weights, score_grad, stat = call(
        far_kernel,
        (
            vmem(HALF, 2 * HEAD_DIM), vmem(PROMPT, ALL), vmem(PROMPT, ALL),
            vmem(16, ANS_LEN, dtype=F32),
        ),
        [VMEM] * 8,
        flops=400_000_000, moved=2_000_000,
    )(bias, own, sibling, queries, grads, exps, moved, stat)

    d_mine = lax.ppermute(d_sib, "c", OTHER_CORE)
    d_own, pair = call(
        mine_kernel,
        (vmem(HALF, 2 * HEAD_DIM, dtype=F32), vmem(HALF, HEAD_DIM)),
        [VMEM] * 7,
        flops=200_000_000, moved=2_000_000,
    )(own, sibling, queries, grads, moved, weights, score_grad)
    back = call(
        post_kernel, bf16(SENDERS, 2, 3 * HEAD_DIM), [VMEM] * 3, limit=4, moved=700_000
    )(d_own, d_mine, pair)
    back, stat = lax.optimization_barrier((back, stat))
    back = lax.all_to_all(back, SAME_CORE, split_axis=0, concat_axis=0, tiled=True)
    a_out, a_dq, a_dk, a_dv = call(
        rest_kernel,
        (
            bf16(ANS_LEN, group), bf16(ANS_LEN, group),
            bf16(ANS_LEN, HEAD_DIM), bf16(ANS_LEN, HEAD_DIM),
        ),
        [SMEM] + [HBM] * 4 + [VMEM] * 5,
        scratch=[
            pltpu.VMEM((ANS_LEN, group), BF16), pltpu.VMEM((ANS_LEN, HEAD_DIM), BF16),
            pltpu.VMEM((ANS_LEN, HEAD_DIM), BF16), pltpu.VMEM((ANS_LEN, group), BF16),
            pltpu.SemaphoreType.DMA((4,)),
        ],
        flops=700_000_000, moved=2_000_000,
    )(
        answer_lengths, in_hbm(answer_q[0]), in_hbm(answer_k[0]), in_hbm(answer_v[0]),
        in_hbm(answer_grad[0]), own, sibling, weights, score_grad, stat,
    )
    p_out, p_dq, p_dk, p_dv = call(
        unpack_kernel, (bf16(2, wide), bf16(2, wide), bf16(2, narrow), bf16(2, narrow)), [VMEM],
        limit=4,
    )(in_vmem(back))
    return (p_out, p_dq, p_dk, p_dv, a_out[None], a_dq[None], a_dk[None], a_dv[None])


def solution(mesh):
    grid = Mesh(mesh.devices.reshape(4, 4, 2, 4, 2), SEQ_AXES + HEAD_AXES)
    rows = P(SEQ_AXES + HEAD_AXES, None)
    answers = P(SEQ_AXES, None, HEAD_AXES)
    return jax.shard_map(
        body,
        mesh=grid,
        in_specs=(rows, rows, rows, rows, P(), answers, answers, answers, answers, P(SEQ_AXES)),
        out_specs=(rows, rows, rows, rows, answers, answers, answers, answers),
        check_vma=False,
    )
```

```python
import math

import jax
import jax.numpy as jnp
from jax import lax
from jax.experimental import pallas as pl
from jax.experimental.pallas import tpu as pltpu
from jax.sharding import Mesh, PartitionSpec as P

HEADS = 40
KV_HEADS = 8
HEAD_DIM = 128
GROUP = HEADS // KV_HEADS
PROMPT = 512
ANS_LEN = 256
HALF = PROMPT // 2
PAIRS = 2 * GROUP
PEERS = 16
SENDERS = 128
ROWS = GROUP * ANS_LEN
ALL = ROWS + SENDERS
NEG = -1e30
SCALING = 1.0 / math.sqrt(HEAD_DIM)
SCALE2 = SCALING / math.log(2.0)
SEQ_AXES = ("y", "zh", "c")
HEAD_AXES = ("x", "zl")
PEER_BITS = ("z0", "x1", "x0", "z2", "z1", "y1", "y0")
PEER_FLIP = 106
OTHER_CORE = [(0, 1), (1, 0)]
VMEM = pl.BlockSpec(memory_space=pltpu.VMEM)
SMEM = pl.BlockSpec(memory_space=pltpu.SMEM)
HBM = pl.BlockSpec(memory_space=pltpu.HBM)
NT = ((1,), (1,))
NN = ((1,), (0,))
BF16 = jnp.bfloat16
F32 = jnp.float32


def dot(a, b, dims):
    return lax.dot_general(a, b, (dims, ((), ())), preferred_element_type=F32)


def cols(i):
    return slice(i * HEAD_DIM, (i + 1) * HEAD_DIM)


def head(n):
    return slice(n * ANS_LEN, min((n + 1) * ANS_LEN, ALL))


def number(peer, names):
    total = 0
    for name in names:
        place = 6 - PEER_BITS.index(name)
        total = total * 2 + (((peer >> place) & 1) ^ ((PEER_FLIP >> place) & 1))
    return total


def group_of(peer):
    return number(peer, ("x1", "x0", "z0"))


def place_of(peer):
    return number(peer, ("y1", "y0", "z2", "z1"))


def row_at(peer, side, row):
    return (place_of(peer) * 2 + side) * 16 + group_of(peer) * 2 + row


def peer_groups():
    return [
        [place_of(peer) * 16 + core * 8 + group_of(peer) for peer in range(SENDERS)]
        for core in range(2)
    ]


def pack_kernel(q_hbm, g_hbm, k_hbm, v_hbm, o_ref, q_ref, g_ref, k_ref, v_ref, sems):
    pairs = ((k_hbm, k_ref), (v_hbm, v_ref), (q_hbm, q_ref), (g_hbm, g_ref))
    copies = [pltpu.make_async_copy(a, b, sems.at[i]) for i, (a, b) in enumerate(pairs)]
    for copy in copies:
        copy.start()
    for copy in copies:
        copy.wait()
    q = q_ref[...].astype(F32)
    g = g_ref[...].astype(F32)
    zero = jnp.zeros((2, HEAD_DIM), BF16)
    rows = [jnp.concatenate([q[r : r + 1], g[r : r + 1]], axis=0).astype(BF16) for r in range(2)]
    for peer in range(SENDERS):
        h = group_of(peer)
        d = place_of(peer)
        o_ref[peer, :, cols(0)] = k_ref[:, cols(h)]
        o_ref[peer, :, cols(1)] = v_ref[:, cols(h)]
        if d < PAIRS:
            pair = rows[d // GROUP][:, cols(h * GROUP + d % GROUP)]
        else:
            pair = zero
        o_ref[peer, :, cols(2)] = pair


def unpack_kernel(x_ref, out_ref, dq_ref, dk_ref, dv_ref):
    peer_at = {(group_of(peer), place_of(peer)): peer for peer in range(SENDERS)}
    for h in range(KV_HEADS):
        total = jnp.zeros((2, 2 * HEAD_DIM), F32)
        for d in range(PEERS):
            total += x_ref[peer_at[h, d], :, : 2 * HEAD_DIM].astype(F32)
        dk_ref[:, cols(h)] = total[:, :HEAD_DIM].astype(BF16)
        dv_ref[:, cols(h)] = total[:, HEAD_DIM:].astype(BF16)
        for n in range(GROUP):
            first = x_ref[peer_at[h, n], :, cols(2)].astype(F32)
            second = x_ref[peer_at[h, GROUP + n], :, cols(2)].astype(F32)
            at = cols(h * GROUP + n)
            out_ref[:, at] = jnp.concatenate([first[:1], second[:1]], axis=0).astype(BF16)
            dq_ref[:, at] = jnp.concatenate([first[1:], second[1:]], axis=0).astype(BF16)


def post_kernel(own_ref, other_ref, pair_ref, o_ref):
    total = (own_ref[...] + other_ref[...].astype(F32)).astype(BF16)
    o_ref[:, :, : 2 * HEAD_DIM] = total.reshape(SENDERS, 2, 2 * HEAD_DIM)
    o_ref[:, :, 2 * HEAD_DIM :] = pair_ref[...].reshape(SENDERS, 2, HEAD_DIM)


def deinterleave(row_axis):
    i = lax.broadcasted_iota(jnp.int32, (HALF, HALF), row_axis)
    j = lax.broadcasted_iota(jnp.int32, (HALF, HALF), 1 - row_axis)
    source = jnp.where(i < SENDERS, 2 * i, 2 * i - HALF + 1)
    return (source == j).astype(BF16)


def seen_by(length):
    u = lax.broadcasted_iota(jnp.int32, (ANS_LEN, ANS_LEN), 0)
    t = lax.broadcasted_iota(jnp.int32, (ANS_LEN, ANS_LEN), 1)
    return (u <= t) & (u < length)


def live_rows(length):
    return lax.broadcasted_iota(jnp.int32, (ANS_LEN, HEAD_DIM), 0) < length


def column_sum(x):
    return jnp.sum(x, axis=0, keepdims=True)


def column_max(x):
    return jnp.max(x, axis=0, keepdims=True)


def own_kernel(
    len_ref, seg_hbm, aq_hbm, ak_hbm, av_hbm, ag_hbm,
    q_ref, g_ref, stat_ref, bias_ref,
    seg_ref, raw_ref, k_ref, v_ref, sems,
):
    pairs = [(seg_hbm, seg_ref), (ak_hbm, k_ref), (av_hbm, v_ref)]
    for n in range(GROUP):
        rows = pl.ds(n * ANS_LEN, ANS_LEN)
        at = pl.ds(n * HEAD_DIM, HEAD_DIM)
        pairs.append((aq_hbm.at[:, at], q_ref.at[rows, :]))
        pairs.append((ag_hbm.at[:, at], raw_ref.at[rows, :]))
    copies = [pltpu.make_async_copy(a, b, sems.at[i]) for i, (a, b) in enumerate(pairs)]
    for copy in copies:
        copy.start()
    length = len_ref[0]
    core = lax.axis_index("c")
    row = jnp.where(lax.axis_index("y") * 4 + lax.axis_index("zh") >= GROUP, 1, 0)

    j = lax.broadcasted_iota(jnp.int32, (PROMPT, 1), 0)
    side = jnp.where(j < HALF, core, 1 - core)
    at = row_at((j & (HALF - 1)) >> 1, side, j & 1)
    key_pick = (at == lax.broadcasted_iota(jnp.int32, (PROMPT, PROMPT), 1)).astype(BF16)
    i = lax.broadcasted_iota(jnp.int32, (SENDERS, 1), 0)
    at = row_at(i, core, row)
    row_pick = (at == lax.broadcasted_iota(jnp.int32, (SENDERS, PROMPT), 1)).astype(BF16)
    copies[0].wait()
    segments = jnp.broadcast_to(seg_ref[...].astype(F32), (SENDERS, PROMPT)).astype(BF16)
    key_segments = dot(key_pick, segments, NT)
    row_segments = dot(segments, row_pick, NT)[:1]
    bias_ref[...] = jnp.where(key_segments <= row_segments, 0.0, NEG)

    seen = seen_by(length)
    live_row = live_rows(length)
    for copy in copies[1:]:
        copy.wait()
    keys = k_ref[...]
    values = v_ref[...]
    for n in range(GROUP):
        grads = raw_ref[head(n)]
        grads = jnp.where(live_row, grads, jnp.zeros_like(grads))
        g_ref[head(n)] = grads
        scores = jnp.where(seen, dot(keys, q_ref[head(n)], NT), NEG)
        top = column_max(scores)
        weights = jnp.exp2(scores * SCALE2 - top * SCALE2)
        stat_ref[n : n + 1] = top
        stat_ref[8 + n : 9 + n] = column_sum(weights)
        stat_ref[16 + n : 17 + n] = column_sum(weights * dot(values, grads, NT))


def near_kernel(
    bias_ref, own_ref, q_ref, g_ref, stat_ref,
    e_ref, far_bias_ref, moved_ref, stat2_ref, q2_ref, g2_ref,
):
    keys = own_ref[:, cols(0)]
    values = own_ref[:, cols(1)]
    moved_ref[...] = dot(deinterleave(0), own_ref[:, cols(2)], NN).astype(BF16)
    far_bias_ref[...] = bias_ref[HALF:]
    q2_ref[...] = q_ref[...]
    g2_ref[...] = g_ref[...]
    for n in range(GROUP + 1):
        if n < GROUP:
            scores = dot(keys, q_ref[head(n)], NT)
            prob_grad = dot(values, g_ref[head(n)], NT)
            old_top = stat_ref[n : n + 1]
            top = jnp.maximum(column_max(scores), old_top)
        else:
            scores = dot(keys, moved_ref[:SENDERS], NT) + bias_ref[:HALF]
            prob_grad = dot(values, moved_ref[SENDERS:], NT)
            top = column_max(scores)
        weights = jnp.exp2(scores * SCALE2 - top * SCALE2)
        total = column_sum(weights)
        moment = column_sum(weights * prob_grad)
        if n < GROUP:
            shift = jnp.exp2((old_top - top) * SCALE2)
            total += stat_ref[8 + n : 9 + n] * shift
            moment += stat_ref[16 + n : 17 + n] * shift
        e_ref[:, head(n)] = weights
        wide = slice(0, weights.shape[1])
        stat2_ref[n : n + 1, wide] = top
        stat2_ref[8 + n : 9 + n, wide] = total
        stat2_ref[16 + n : 17 + n, wide] = moment


def far_kernel(
    bias_ref, own_ref, sib_ref, q_ref, g_ref, e_ref, moved_ref, stat_ref,
    dsib_ref, w_ref, ds_ref, stat2_ref,
):
    keys = sib_ref[:, cols(0)]
    values = sib_ref[:, cols(1)]
    near_values = own_ref[:, cols(1)]
    for n in range(GROUP + 1):
        if n < GROUP:
            scores = dot(keys, q_ref[head(n)], NT)
            grads = g_ref[head(n)]
        else:
            scores = dot(keys, moved_ref[:SENDERS], NT) + bias_ref[...]
            grads = moved_ref[SENDERS:]
        prob_grad = dot(values, grads, NT)
        wide = slice(0, scores.shape[1])
        old_top = stat_ref[n : n + 1, wide]
        top = jnp.maximum(column_max(scores), old_top)
        shift = jnp.exp2((old_top - top) * SCALE2)
        weights = jnp.exp2(scores * SCALE2 - top * SCALE2)
        total = column_sum(weights) + stat_ref[8 + n : 9 + n, wide] * shift
        moment = column_sum(weights * prob_grad) + stat_ref[16 + n : 17 + n, wide] * shift
        inverse = 1.0 / total
        delta = moment * inverse
        if n < GROUP:
            stat2_ref[n : n + 1] = top * SCALE2 + jnp.log2(total)
            stat2_ref[8 + n : 9 + n] = delta
        weights = weights * inverse
        w_ref[HALF:, head(n)] = weights.astype(BF16)
        ds_ref[HALF:, head(n)] = (weights * (prob_grad - delta)).astype(BF16)
        weights = e_ref[:, head(n)] * (shift * inverse)
        w_ref[:HALF, head(n)] = weights.astype(BF16)
        ds_ref[:HALF, head(n)] = (weights * (dot(near_values, grads, NT) - delta)).astype(BF16)
    dk, dv = key_terms(ds_ref[HALF:], w_ref[HALF:], q_ref, g_ref, moved_ref)
    dsib_ref[:, cols(0)] = dk.astype(BF16)
    dsib_ref[:, cols(1)] = dv.astype(BF16)


def key_terms(score_grad, weights, q_ref, g_ref, moved_ref):
    dk = dot(score_grad[:, :ROWS], q_ref[...], NN)
    dk += dot(score_grad[:, ROWS:], moved_ref[:SENDERS], NN)
    dv = dot(weights[:, :ROWS], g_ref[...], NN)
    dv += dot(weights[:, ROWS:], moved_ref[SENDERS:], NN)
    return dk * SCALING, dv


def mine_kernel(
    own_ref, sib_ref, q_ref, g_ref, moved_ref, w_ref, ds_ref, down_ref, pair_ref
):
    dk, dv = key_terms(ds_ref[:HALF], w_ref[:HALF], q_ref, g_ref, moved_ref)
    down_ref[:, cols(0)] = dk
    down_ref[:, cols(1)] = dv
    results = []
    for part, x_ref, factor in ((1, w_ref, 1.0), (0, ds_ref, SCALING)):
        turned = dot(own_ref[:, cols(part)].T, x_ref[:HALF, head(GROUP)], NN)
        turned += dot(sib_ref[:, cols(part)].T, x_ref[HALF:, head(GROUP)], NN)
        results.append((turned * factor).T)
    both = jnp.concatenate(results, axis=0).astype(BF16)
    pair_ref[...] = dot(deinterleave(1), both, NN).astype(BF16)


def rest_kernel(
    len_ref, aq_hbm, ak_hbm, av_hbm, ag_hbm, own_ref, sib_ref, w_ref, ds_ref, stat_ref,
    aout_ref, adq_ref, adk_ref, adv_ref, q_ref, k_ref, v_ref, g_ref, sems,
):
    pairs = ((aq_hbm, q_ref), (ak_hbm, k_ref), (av_hbm, v_ref), (ag_hbm, g_ref))
    copies = [pltpu.make_async_copy(a, b, sems.at[i]) for i, (a, b) in enumerate(pairs)]
    for copy in copies:
        copy.start()
    for copy in copies:
        copy.wait()
    length = len_ref[0]
    seen = seen_by(length)
    live_row = live_rows(length)
    keys = k_ref[...]
    values = v_ref[...]
    keys_t = keys.T
    values_t = values.T
    prompt_keys_t = jnp.concatenate([own_ref[:, cols(0)], sib_ref[:, cols(0)]], axis=0).T
    prompt_values_t = jnp.concatenate([own_ref[:, cols(1)], sib_ref[:, cols(1)]], axis=0).T
    dk = jnp.zeros((ANS_LEN, HEAD_DIM), F32)
    dv = jnp.zeros((ANS_LEN, HEAD_DIM), F32)
    for n in range(GROUP):
        queries = q_ref[:, cols(n)]
        grads = g_ref[:, cols(n)]
        grads = jnp.where(live_row, grads, jnp.zeros_like(grads))
        scores = jnp.where(seen, dot(keys, queries, NT), NEG)
        weights = jnp.exp2(scores * SCALE2 - stat_ref[n : n + 1])
        weights_low = weights.astype(BF16)
        product = dot(values, grads, NT) - stat_ref[8 + n : 9 + n]
        score_grad = (weights * product).astype(BF16)
        out_t = dot(prompt_values_t, w_ref[:, head(n)], NN) + dot(values_t, weights_low, NN)
        dq_t = dot(prompt_keys_t, ds_ref[:, head(n)], NN) + dot(keys_t, score_grad, NN)
        aout_ref[:, cols(n)] = jnp.where(live_row, out_t.T, 0.0).astype(BF16)
        adq_ref[:, cols(n)] = (dq_t * SCALING).T.astype(BF16)
        dk += dot(score_grad, queries, NN)
        dv += dot(weights_low, grads, NN)
    adk_ref[...] = (dk * SCALING).astype(BF16)
    adv_ref[...] = dv.astype(BF16)


def call(kernel, out_shape, specs, scratch=(), flops=0, moved=0, limit=16):
    return pl.pallas_call(
        kernel,
        out_shape=out_shape,
        in_specs=specs,
        out_specs=jax.tree.map(lambda _: VMEM, out_shape),
        scratch_shapes=list(scratch),
        cost_estimate=pl.CostEstimate(flops=flops, bytes_accessed=moved, transcendentals=0),
        compiler_params=pltpu.CompilerParams(vmem_limit_bytes=limit * 1024 * 1024),
    )


def bf16(*shape):
    return jax.ShapeDtypeStruct(shape, BF16)


def vmem(*shape, dtype=BF16):
    return pltpu.VMEM(shape, dtype)


def in_hbm(x):
    return pltpu.with_memory_space_constraint(x, pltpu.HBM)


def in_vmem(x):
    return pltpu.with_memory_space_constraint(x, pltpu.VMEM)


def exchange(x):
    return lax.all_to_all(
        x, SEQ_AXES + HEAD_AXES, split_axis=0, concat_axis=0, tiled=True,
        axis_index_groups=peer_groups(),
    )


def body(
    prompt_q, prompt_k, prompt_v, prompt_grad, segment_ids,
    answer_q, answer_k, answer_v, answer_grad, answer_lengths,
):
    wide = HEADS * HEAD_DIM
    narrow = KV_HEADS * HEAD_DIM
    group = GROUP * HEAD_DIM
    packed = call(
        pack_kernel,
        bf16(SENDERS, 2, 3 * HEAD_DIM),
        [HBM] * 4,
        scratch=[
            pltpu.VMEM((2, wide), BF16), pltpu.VMEM((2, wide), BF16),
            pltpu.VMEM((2, narrow), BF16), pltpu.VMEM((2, narrow), BF16),
            pltpu.SemaphoreType.DMA((4,)),
        ],
        limit=4,
    )(in_hbm(prompt_q), in_hbm(prompt_grad), in_hbm(prompt_k), in_hbm(prompt_v))
    packed, answer_q = lax.optimization_barrier((packed, answer_q))
    own = exchange(packed)
    own = own.reshape(HALF, 3 * HEAD_DIM)

    queries, grads, stat, bias = call(
        own_kernel,
        (
            vmem(ROWS, HEAD_DIM), vmem(ROWS, HEAD_DIM), vmem(24, ANS_LEN, dtype=F32),
            vmem(PROMPT, SENDERS, dtype=F32),
        ),
        [SMEM] + [HBM] * 5,
        scratch=[
            pltpu.VMEM((1, PROMPT), jnp.int32), pltpu.VMEM((ROWS, HEAD_DIM), BF16),
            pltpu.VMEM((ANS_LEN, HEAD_DIM), BF16), pltpu.VMEM((ANS_LEN, HEAD_DIM), BF16),
            pltpu.SemaphoreType.DMA((3 + 2 * GROUP,)),
        ],
        flops=400_000_000, moved=2_000_000,
    )(
        answer_lengths, in_hbm(segment_ids.reshape(1, PROMPT)), in_hbm(answer_q[0]),
        in_hbm(answer_k[0]), in_hbm(answer_v[0]), in_hbm(answer_grad[0]),
    )
    own, stat = lax.optimization_barrier((own, stat))
    sibling = lax.ppermute(own, "c", OTHER_CORE)
    exps, bias, moved, stat, queries, grads = call(
        near_kernel,
        (
            vmem(HALF, ALL, dtype=F32), vmem(HALF, SENDERS, dtype=F32), vmem(HALF, HEAD_DIM),
            vmem(24, ANS_LEN, dtype=F32), vmem(ROWS, HEAD_DIM), vmem(ROWS, HEAD_DIM),
        ),
        [VMEM] * 5,
        flops=200_000_000, moved=2_000_000,
    )(bias, own, queries, grads, stat)
    d_sib, weights, score_grad, stat = call(
        far_kernel,
        (
            vmem(HALF, 2 * HEAD_DIM), vmem(PROMPT, ALL), vmem(PROMPT, ALL),
            vmem(16, ANS_LEN, dtype=F32),
        ),
        [VMEM] * 8,
        flops=400_000_000, moved=2_000_000,
    )(bias, own, sibling, queries, grads, exps, moved, stat)

    d_mine = lax.ppermute(d_sib, "c", OTHER_CORE)
    d_own, pair = call(
        mine_kernel,
        (vmem(HALF, 2 * HEAD_DIM, dtype=F32), vmem(HALF, HEAD_DIM)),
        [VMEM] * 7,
        flops=200_000_000, moved=2_000_000,
    )(own, sibling, queries, grads, moved, weights, score_grad)
    back = call(
        post_kernel, bf16(SENDERS, 2, 3 * HEAD_DIM), [VMEM] * 3, limit=4, moved=700_000
    )(d_own, d_mine, pair)
    back, stat = lax.optimization_barrier((back, stat))
    back = exchange(back)
    a_out, a_dq, a_dk, a_dv = call(
        rest_kernel,
        (
            bf16(ANS_LEN, group), bf16(ANS_LEN, group),
            bf16(ANS_LEN, HEAD_DIM), bf16(ANS_LEN, HEAD_DIM),
        ),
        [SMEM] + [HBM] * 4 + [VMEM] * 5,
        scratch=[
            pltpu.VMEM((ANS_LEN, group), BF16), pltpu.VMEM((ANS_LEN, HEAD_DIM), BF16),
            pltpu.VMEM((ANS_LEN, HEAD_DIM), BF16), pltpu.VMEM((ANS_LEN, group), BF16),
            pltpu.SemaphoreType.DMA((4,)),
        ],
        flops=700_000_000, moved=2_000_000,
    )(
        answer_lengths, in_hbm(answer_q[0]), in_hbm(answer_k[0]), in_hbm(answer_v[0]),
        in_hbm(answer_grad[0]), own, sibling, weights, score_grad, stat,
    )
    p_out, p_dq, p_dk, p_dv = call(
        unpack_kernel, (bf16(2, wide), bf16(2, wide), bf16(2, narrow), bf16(2, narrow)), [VMEM],
        limit=4,
    )(in_vmem(back))
    return (p_out, p_dq, p_dk, p_dv, a_out[None], a_dq[None], a_dk[None], a_dv[None])


def solution(mesh):
    grid = Mesh(mesh.devices.reshape(4, 4, 2, 4, 2), SEQ_AXES + HEAD_AXES)
    rows = P(SEQ_AXES + HEAD_AXES, None)
    answers = P(SEQ_AXES, None, HEAD_AXES)
    return jax.shard_map(
        body,
        mesh=grid,
        in_specs=(rows, rows, rows, rows, P(), answers, answers, answers, answers, P(SEQ_AXES)),
        out_specs=(rows, rows, rows, rows, answers, answers, answers, answers),
        check_vma=False,
    )
```

```python
import math

import jax
import jax.numpy as jnp
from jax import lax
from jax.experimental import pallas as pl
from jax.experimental.pallas import tpu as pltpu
from jax.sharding import Mesh, PartitionSpec as P

HEADS = 40
KV_HEADS = 8
HEAD_DIM = 128
GROUP = HEADS // KV_HEADS
PROMPT = 512
ANS_LEN = 256
HALF = PROMPT // 2
PAIRS = 2 * GROUP
PEERS = 16
SENDERS = 128
ROWS = GROUP * ANS_LEN
ALL = ROWS + SENDERS
NEG = -1e30
SCALING = 1.0 / math.sqrt(HEAD_DIM)
SCALE2 = SCALING / math.log(2.0)
SEQ_AXES = ("y", "zh", "c")
HEAD_AXES = ("x", "zl")
PEER_BITS = ("z0", "x1", "x0", "z2", "z1", "y1", "y0")
PEER_FLIP = 106
OTHER_CORE = [(0, 1), (1, 0)]
VMEM = pl.BlockSpec(memory_space=pltpu.VMEM)
SMEM = pl.BlockSpec(memory_space=pltpu.SMEM)
HBM = pl.BlockSpec(memory_space=pltpu.HBM)
NT = ((1,), (1,))
NN = ((1,), (0,))
BF16 = jnp.bfloat16
F32 = jnp.float32


def dot(a, b, dims):
    return lax.dot_general(a, b, (dims, ((), ())), preferred_element_type=F32)


def cols(i):
    return slice(i * HEAD_DIM, (i + 1) * HEAD_DIM)


def head(n):
    return slice(n * ANS_LEN, min((n + 1) * ANS_LEN, ALL))


def number(peer, names):
    total = 0
    for name in names:
        place = 6 - PEER_BITS.index(name)
        total = total * 2 + (((peer >> place) & 1) ^ ((PEER_FLIP >> place) & 1))
    return total


def group_of(peer):
    return number(peer, ("x1", "x0", "z0"))


def place_of(peer):
    return number(peer, ("y1", "y0", "z2", "z1"))


def row_at(peer, side, row):
    return (place_of(peer) * 2 + side) * 16 + group_of(peer) * 2 + row


def peer_groups():
    return [
        [place_of(peer) * 16 + core * 8 + group_of(peer) for peer in range(SENDERS)]
        for core in range(2)
    ]


def pack_kernel(q_hbm, g_hbm, k_hbm, v_hbm, o_ref, q_ref, g_ref, k_ref, v_ref, sems):
    pairs = ((k_hbm, k_ref), (v_hbm, v_ref), (q_hbm, q_ref), (g_hbm, g_ref))
    copies = [pltpu.make_async_copy(a, b, sems.at[i]) for i, (a, b) in enumerate(pairs)]
    for copy in copies:
        copy.start()
    for copy in copies:
        copy.wait()
    q = q_ref[...].astype(F32)
    g = g_ref[...].astype(F32)
    zero = jnp.zeros((2, HEAD_DIM), BF16)
    rows = [jnp.concatenate([q[r : r + 1], g[r : r + 1]], axis=0).astype(BF16) for r in range(2)]
    for peer in range(SENDERS):
        h = group_of(peer)
        d = place_of(peer)
        o_ref[peer, :, cols(0)] = k_ref[:, cols(h)]
        o_ref[peer, :, cols(1)] = v_ref[:, cols(h)]
        if d < PAIRS:
            pair = rows[d // GROUP][:, cols(h * GROUP + d % GROUP)]
        else:
            pair = zero
        o_ref[peer, :, cols(2)] = pair


def unpack_kernel(x_ref, out_ref, dq_ref, dk_ref, dv_ref):
    peer_at = {(group_of(peer), place_of(peer)): peer for peer in range(SENDERS)}
    for h in range(KV_HEADS):
        total = jnp.zeros((2, 2 * HEAD_DIM), F32)
        for d in range(PEERS):
            total += x_ref[peer_at[h, d], :, : 2 * HEAD_DIM].astype(F32)
        dk_ref[:, cols(h)] = total[:, :HEAD_DIM].astype(BF16)
        dv_ref[:, cols(h)] = total[:, HEAD_DIM:].astype(BF16)
        for n in range(GROUP):
            first = x_ref[peer_at[h, n], :, cols(2)].astype(F32)
            second = x_ref[peer_at[h, GROUP + n], :, cols(2)].astype(F32)
            at = cols(h * GROUP + n)
            out_ref[:, at] = jnp.concatenate([first[:1], second[:1]], axis=0).astype(BF16)
            dq_ref[:, at] = jnp.concatenate([first[1:], second[1:]], axis=0).astype(BF16)


def post_kernel(own_ref, other_ref, pair_ref, o_ref):
    total = (own_ref[...] + other_ref[...].astype(F32)).astype(BF16)
    o_ref[:, :, : 2 * HEAD_DIM] = total.reshape(SENDERS, 2, 2 * HEAD_DIM)
    o_ref[:, :, 2 * HEAD_DIM :] = pair_ref[...].reshape(SENDERS, 2, HEAD_DIM)


def deinterleave(row_axis):
    i = lax.broadcasted_iota(jnp.int32, (HALF, HALF), row_axis)
    j = lax.broadcasted_iota(jnp.int32, (HALF, HALF), 1 - row_axis)
    source = jnp.where(i < SENDERS, 2 * i, 2 * i - HALF + 1)
    return (source == j).astype(BF16)


def seen_by(length):
    u = lax.broadcasted_iota(jnp.int32, (ANS_LEN, ANS_LEN), 0)
    t = lax.broadcasted_iota(jnp.int32, (ANS_LEN, ANS_LEN), 1)
    return (u <= t) & (u < length)


def live_rows(length):
    return lax.broadcasted_iota(jnp.int32, (ANS_LEN, HEAD_DIM), 0) < length


def column_sum(x):
    return jnp.sum(x, axis=0, keepdims=True)


def column_max(x):
    return jnp.max(x, axis=0, keepdims=True)


def own_kernel(
    len_ref, seg_hbm, aq_hbm, ak_hbm, av_hbm, ag_hbm,
    q_ref, g_ref, stat_ref, bias_ref,
    seg_ref, raw_ref, k_ref, v_ref, sems,
):
    pairs = [(seg_hbm, seg_ref), (ak_hbm, k_ref), (av_hbm, v_ref)]
    for n in range(GROUP):
        rows = pl.ds(n * ANS_LEN, ANS_LEN)
        at = pl.ds(n * HEAD_DIM, HEAD_DIM)
        pairs.append((aq_hbm.at[:, at], q_ref.at[rows, :]))
        pairs.append((ag_hbm.at[:, at], raw_ref.at[rows, :]))
    copies = [pltpu.make_async_copy(a, b, sems.at[i]) for i, (a, b) in enumerate(pairs)]
    for copy in copies:
        copy.start()
    length = len_ref[0]
    core = lax.axis_index("c")
    row = jnp.where(lax.axis_index("y") * 4 + lax.axis_index("zh") >= GROUP, 1, 0)

    j = lax.broadcasted_iota(jnp.int32, (PROMPT, 1), 0)
    side = jnp.where(j < HALF, core, 1 - core)
    at = row_at((j & (HALF - 1)) >> 1, side, j & 1)
    key_pick = (at == lax.broadcasted_iota(jnp.int32, (PROMPT, PROMPT), 1)).astype(BF16)
    i = lax.broadcasted_iota(jnp.int32, (SENDERS, 1), 0)
    at = row_at(i, core, row)
    row_pick = (at == lax.broadcasted_iota(jnp.int32, (SENDERS, PROMPT), 1)).astype(BF16)
    copies[0].wait()
    segments = jnp.broadcast_to(seg_ref[...].astype(F32), (SENDERS, PROMPT)).astype(BF16)
    key_segments = dot(key_pick, segments, NT)
    row_segments = dot(segments, row_pick, NT)[:1]
    bias_ref[...] = jnp.where(key_segments <= row_segments, 0.0, NEG)

    seen = seen_by(length)
    live_row = live_rows(length)
    for copy in copies[1:]:
        copy.wait()
    keys = k_ref[...]
    values = v_ref[...]
    for n in range(GROUP):
        grads = raw_ref[head(n)]
        grads = jnp.where(live_row, grads, jnp.zeros_like(grads))
        g_ref[head(n)] = grads
        scores = jnp.where(seen, dot(keys, q_ref[head(n)], NT), NEG)
        top = column_max(scores)
        weights = jnp.exp2(scores * SCALE2 - top * SCALE2)
        stat_ref[0:1, head(n)] = top
        stat_ref[1:2, head(n)] = column_sum(weights)
        stat_ref[2:3, head(n)] = column_sum(weights * dot(values, grads, NT))


def near_kernel(
    bias_ref, own_ref, q_ref, g_ref, stat_ref,
    e_ref, far_bias_ref, stat2_ref, q2_ref, g2_ref,
):
    keys = own_ref[:, cols(0)]
    values = own_ref[:, cols(1)]
    moved = dot(deinterleave(0), own_ref[:, cols(2)], NN).astype(BF16)
    far_bias_ref[...] = bias_ref[HALF:]
    q2_ref[:ROWS] = q_ref[...]
    g2_ref[:ROWS] = g_ref[...]
    q2_ref[ROWS:] = moved[:SENDERS]
    g2_ref[ROWS:] = moved[SENDERS:]
    for n in range(GROUP + 1):
        if n < GROUP:
            scores = dot(keys, q_ref[head(n)], NT)
            prob_grad = dot(values, g_ref[head(n)], NT)
            old_top = stat_ref[0:1, head(n)]
            top = jnp.maximum(column_max(scores), old_top)
        else:
            scores = dot(keys, moved[:SENDERS], NT) + bias_ref[:HALF]
            prob_grad = dot(values, moved[SENDERS:], NT)
            top = column_max(scores)
        weights = jnp.exp2(scores * SCALE2 - top * SCALE2)
        total = column_sum(weights)
        moment = column_sum(weights * prob_grad)
        if n < GROUP:
            shift = jnp.exp2((old_top - top) * SCALE2)
            total += stat_ref[1:2, head(n)] * shift
            moment += stat_ref[2:3, head(n)] * shift
        e_ref[:, head(n)] = weights
        stat2_ref[0:1, head(n)] = top
        stat2_ref[1:2, head(n)] = total
        stat2_ref[2:3, head(n)] = moment


def far_kernel(
    bias_ref, sib_ref, q_ref, g_ref, stat_ref, dsib_ref, w_ref, ds_ref, stat2_ref
):
    scores = dot(sib_ref[:, cols(0)], q_ref[...], NT)
    scores = jnp.concatenate([scores[:, :ROWS], scores[:, ROWS:] + bias_ref[...]], axis=1)
    prob_grad = dot(sib_ref[:, cols(1)], g_ref[...], NT)
    old_top = stat_ref[0:1]
    top = jnp.maximum(column_max(scores), old_top)
    shift = jnp.exp2((old_top - top) * SCALE2)
    weights = jnp.exp2(scores * SCALE2 - top * SCALE2)
    total = column_sum(weights) + stat_ref[1:2] * shift
    moment = column_sum(weights * prob_grad) + stat_ref[2:3] * shift
    inverse = 1.0 / total
    delta = moment * inverse
    stat2_ref[0:1] = top * SCALE2 + jnp.log2(total)
    stat2_ref[1:2] = delta
    stat2_ref[2:3] = shift * inverse
    weights = weights * inverse
    w_ref[...] = weights.astype(BF16)
    ds_ref[...] = (weights * (prob_grad - delta)).astype(BF16)
    dsib_ref[:, cols(0)] = (dot(ds_ref[...], q_ref[...], NN) * SCALING).astype(BF16)
    dsib_ref[:, cols(1)] = dot(w_ref[...], g_ref[...], NN).astype(BF16)


def mine_kernel(
    own_ref, sib_ref, q_ref, g_ref, e_ref, stat_ref, wsib_ref, dssib_ref,
    down_ref, pair_ref, w_ref, ds_ref,
):
    prob_grad = dot(own_ref[:, cols(1)], g_ref[...], NT)
    weights = e_ref[...] * stat_ref[2:3]
    w_ref[...] = weights.astype(BF16)
    ds_ref[...] = (weights * (prob_grad - stat_ref[1:2])).astype(BF16)
    down_ref[:, cols(0)] = dot(ds_ref[...], q_ref[...], NN) * SCALING
    down_ref[:, cols(1)] = dot(w_ref[...], g_ref[...], NN)
    results = []
    for part, near_ref, far_ref, factor in (
        (1, w_ref, wsib_ref, 1.0), (0, ds_ref, dssib_ref, SCALING)
    ):
        turned = dot(own_ref[:, cols(part)].T, near_ref[:, head(GROUP)], NN)
        turned += dot(sib_ref[:, cols(part)].T, far_ref[:, head(GROUP)], NN)
        results.append((turned * factor).T)
    both = jnp.concatenate(results, axis=0).astype(BF16)
    pair_ref[...] = dot(deinterleave(1), both, NN).astype(BF16)


def rest_kernel(
    len_ref, aq_hbm, ak_hbm, av_hbm, ag_hbm, own_ref, sib_ref,
    w_ref, ds_ref, wsib_ref, dssib_ref, stat_ref,
    aout_ref, adq_ref, adk_ref, adv_ref, q_ref, k_ref, v_ref, g_ref, out_ref, dq_ref, sems,
):
    pairs = ((aq_hbm, q_ref), (ak_hbm, k_ref), (av_hbm, v_ref), (ag_hbm, g_ref))
    copies = [pltpu.make_async_copy(a, b, sems.at[i]) for i, (a, b) in enumerate(pairs)]
    for copy in copies:
        copy.start()
    length = len_ref[0]
    seen = seen_by(length)
    live_row = live_rows(length)
    for part, near_ref, far_ref, sum_ref in (
        (1, w_ref, wsib_ref, out_ref), (0, ds_ref, dssib_ref, dq_ref)
    ):
        sum_ref[...] = dot(own_ref[:, cols(part)].T, near_ref[:, :ROWS], NN)
        sum_ref[...] += dot(sib_ref[:, cols(part)].T, far_ref[:, :ROWS], NN)
    for copy in copies:
        copy.wait()
    keys = k_ref[...]
    values = v_ref[...]
    keys_t = keys.T
    values_t = values.T
    dk = jnp.zeros((ANS_LEN, HEAD_DIM), F32)
    dv = jnp.zeros((ANS_LEN, HEAD_DIM), F32)
    for n in range(GROUP):
        queries = q_ref[:, cols(n)]
        grads = g_ref[:, cols(n)]
        grads = jnp.where(live_row, grads, jnp.zeros_like(grads))
        scores = jnp.where(seen, dot(keys, queries, NT), NEG)
        weights = jnp.exp2(scores * SCALE2 - stat_ref[0:1, head(n)])
        weights_low = weights.astype(BF16)
        product = dot(values, grads, NT) - stat_ref[1:2, head(n)]
        score_grad = (weights * product).astype(BF16)
        out_t = out_ref[:, head(n)] + dot(values_t, weights_low, NN)
        dq_t = dq_ref[:, head(n)] + dot(keys_t, score_grad, NN)
        aout_ref[:, cols(n)] = jnp.where(live_row, out_t.T, 0.0).astype(BF16)
        adq_ref[:, cols(n)] = (dq_t * SCALING).T.astype(BF16)
        dk += dot(score_grad, queries, NN)
        dv += dot(weights_low, grads, NN)
    adk_ref[...] = (dk * SCALING).astype(BF16)
    adv_ref[...] = dv.astype(BF16)


def call(kernel, out_shape, specs, scratch=(), flops=0, moved=0, limit=16):
    return pl.pallas_call(
        kernel,
        out_shape=out_shape,
        in_specs=specs,
        out_specs=jax.tree.map(lambda _: VMEM, out_shape),
        scratch_shapes=list(scratch),
        cost_estimate=pl.CostEstimate(flops=flops, bytes_accessed=moved, transcendentals=0),
        compiler_params=pltpu.CompilerParams(vmem_limit_bytes=limit * 1024 * 1024),
    )


def bf16(*shape):
    return jax.ShapeDtypeStruct(shape, BF16)


def vmem(*shape, dtype=BF16):
    return pltpu.VMEM(shape, dtype)


def in_hbm(x):
    return pltpu.with_memory_space_constraint(x, pltpu.HBM)


def in_vmem(x):
    return pltpu.with_memory_space_constraint(x, pltpu.VMEM)


def exchange(x):
    return lax.all_to_all(
        x, SEQ_AXES + HEAD_AXES, split_axis=0, concat_axis=0, tiled=True,
        axis_index_groups=peer_groups(),
    )


def body(
    prompt_q, prompt_k, prompt_v, prompt_grad, segment_ids,
    answer_q, answer_k, answer_v, answer_grad, answer_lengths,
):
    wide = HEADS * HEAD_DIM
    narrow = KV_HEADS * HEAD_DIM
    group = GROUP * HEAD_DIM
    packed = call(
        pack_kernel,
        bf16(SENDERS, 2, 3 * HEAD_DIM),
        [HBM] * 4,
        scratch=[
            pltpu.VMEM((2, wide), BF16), pltpu.VMEM((2, wide), BF16),
            pltpu.VMEM((2, narrow), BF16), pltpu.VMEM((2, narrow), BF16),
            pltpu.SemaphoreType.DMA((4,)),
        ],
        limit=4,
    )(in_hbm(prompt_q), in_hbm(prompt_grad), in_hbm(prompt_k), in_hbm(prompt_v))
    packed, answer_q = lax.optimization_barrier((packed, answer_q))
    own = exchange(packed)
    own = own.reshape(HALF, 3 * HEAD_DIM)

    queries, grads, stat, bias = call(
        own_kernel,
        (
            vmem(ROWS, HEAD_DIM), vmem(ROWS, HEAD_DIM), vmem(8, ROWS, dtype=F32),
            vmem(PROMPT, SENDERS, dtype=F32),
        ),
        [SMEM] + [HBM] * 5,
        scratch=[
            pltpu.VMEM((1, PROMPT), jnp.int32), pltpu.VMEM((ROWS, HEAD_DIM), BF16),
            pltpu.VMEM((ANS_LEN, HEAD_DIM), BF16), pltpu.VMEM((ANS_LEN, HEAD_DIM), BF16),
            pltpu.SemaphoreType.DMA((3 + 2 * GROUP,)),
        ],
        flops=400_000_000, moved=2_000_000,
    )(
        answer_lengths, in_hbm(segment_ids.reshape(1, PROMPT)), in_hbm(answer_q[0]),
        in_hbm(answer_k[0]), in_hbm(answer_v[0]), in_hbm(answer_grad[0]),
    )
    own, stat = lax.optimization_barrier((own, stat))
    sibling = lax.ppermute(own, "c", OTHER_CORE)
    exps, bias, stat, queries, grads = call(
        near_kernel,
        (
            vmem(HALF, ALL, dtype=F32), vmem(HALF, SENDERS, dtype=F32),
            vmem(8, ALL, dtype=F32), vmem(ALL, HEAD_DIM), vmem(ALL, HEAD_DIM),
        ),
        [VMEM] * 5,
        flops=200_000_000, moved=2_000_000,
    )(bias, own, queries, grads, stat)
    d_sib, far_w, far_ds, stat = call(
        far_kernel,
        (
            vmem(HALF, 2 * HEAD_DIM), vmem(HALF, ALL), vmem(HALF, ALL),
            vmem(8, ALL, dtype=F32),
        ),
        [VMEM] * 5,
        flops=400_000_000, moved=2_000_000,
    )(bias, sibling, queries, grads, stat)

    d_mine = lax.ppermute(d_sib, "c", OTHER_CORE)
    d_own, pair, near_w, near_ds = call(
        mine_kernel,
        (
            vmem(HALF, 2 * HEAD_DIM, dtype=F32), vmem(HALF, HEAD_DIM),
            vmem(HALF, ALL), vmem(HALF, ALL),
        ),
        [VMEM] * 8,
        flops=200_000_000, moved=2_000_000,
    )(own, sibling, queries, grads, exps, stat, far_w, far_ds)
    back = call(
        post_kernel, bf16(SENDERS, 2, 3 * HEAD_DIM), [VMEM] * 3, limit=4, moved=700_000
    )(d_own, d_mine, pair)
    back, stat = lax.optimization_barrier((back, stat))
    back = exchange(back)
    a_out, a_dq, a_dk, a_dv = call(
        rest_kernel,
        (
            bf16(ANS_LEN, group), bf16(ANS_LEN, group),
            bf16(ANS_LEN, HEAD_DIM), bf16(ANS_LEN, HEAD_DIM),
        ),
        [SMEM] + [HBM] * 4 + [VMEM] * 7,
        scratch=[
            pltpu.VMEM((ANS_LEN, group), BF16), pltpu.VMEM((ANS_LEN, HEAD_DIM), BF16),
            pltpu.VMEM((ANS_LEN, HEAD_DIM), BF16), pltpu.VMEM((ANS_LEN, group), BF16),
            pltpu.VMEM((HEAD_DIM, ROWS), F32), pltpu.VMEM((HEAD_DIM, ROWS), F32),
            pltpu.SemaphoreType.DMA((4,)),
        ],
        flops=700_000_000, moved=2_000_000,
    )(
        answer_lengths, in_hbm(answer_q[0]), in_hbm(answer_k[0]), in_hbm(answer_v[0]),
        in_hbm(answer_grad[0]), own, sibling, near_w, near_ds, far_w, far_ds, stat,
    )
    p_out, p_dq, p_dk, p_dv = call(
        unpack_kernel, (bf16(2, wide), bf16(2, wide), bf16(2, narrow), bf16(2, narrow)), [VMEM],
        limit=4,
    )(in_vmem(back))
    return (p_out, p_dq, p_dk, p_dv, a_out[None], a_dq[None], a_dk[None], a_dv[None])


def solution(mesh):
    grid = Mesh(mesh.devices.reshape(4, 4, 2, 4, 2), SEQ_AXES + HEAD_AXES)
    rows = P(SEQ_AXES + HEAD_AXES, None)
    answers = P(SEQ_AXES, None, HEAD_AXES)
    return jax.shard_map(
        body,
        mesh=grid,
        in_specs=(rows, rows, rows, rows, P(), answers, answers, answers, answers, P(SEQ_AXES)),
        out_specs=(rows, rows, rows, rows, answers, answers, answers, answers),
        check_vma=False,
    )
```

```python
import math

import jax
import jax.numpy as jnp
from jax import lax
from jax.experimental import pallas as pl
from jax.experimental.pallas import tpu as pltpu
from jax.sharding import Mesh, PartitionSpec as P

HEADS = 40
KV_HEADS = 8
HEAD_DIM = 128
GROUP = HEADS // KV_HEADS
PROMPT = 512
ANS_LEN = 256
HALF = PROMPT // 2
PAIRS = 2 * GROUP
PEERS = 16
SENDERS = 128
ROWS = GROUP * ANS_LEN
ALL = ROWS + SENDERS
NEG = -1e30
SCALING = 1.0 / math.sqrt(HEAD_DIM)
SCALE2 = SCALING / math.log(2.0)
SEQ_AXES = ("y", "zh", "c")
HEAD_AXES = ("x", "zl")
PEER_BITS = ("z0", "x1", "x0", "z2", "z1", "y1", "y0")
PEER_FLIP = 106
OTHER_CORE = [(0, 1), (1, 0)]
VMEM = pl.BlockSpec(memory_space=pltpu.VMEM)
SMEM = pl.BlockSpec(memory_space=pltpu.SMEM)
HBM = pl.BlockSpec(memory_space=pltpu.HBM)
NT = ((1,), (1,))
NN = ((1,), (0,))
BF16 = jnp.bfloat16
F32 = jnp.float32


def dot(a, b, dims):
    return lax.dot_general(a, b, (dims, ((), ())), preferred_element_type=F32)


def cols(i):
    return slice(i * HEAD_DIM, (i + 1) * HEAD_DIM)


def head(n):
    return slice(n * ANS_LEN, min((n + 1) * ANS_LEN, ALL))


def number(peer, names):
    total = 0
    for name in names:
        place = 6 - PEER_BITS.index(name)
        total = total * 2 + (((peer >> place) & 1) ^ ((PEER_FLIP >> place) & 1))
    return total


def group_of(peer):
    return number(peer, ("x1", "x0", "z0"))


def place_of(peer):
    return number(peer, ("y1", "y0", "z2", "z1"))


def row_at(peer, side, row):
    return (place_of(peer) * 2 + side) * 16 + group_of(peer) * 2 + row


def peer_groups():
    return [
        [place_of(peer) * 16 + core * 8 + group_of(peer) for peer in range(SENDERS)]
        for core in range(2)
    ]


def pack_kernel(q_hbm, g_hbm, k_hbm, v_hbm, o_ref, q_ref, g_ref, k_ref, v_ref, sems):
    pairs = ((k_hbm, k_ref), (v_hbm, v_ref), (q_hbm, q_ref), (g_hbm, g_ref))
    copies = [pltpu.make_async_copy(a, b, sems.at[i]) for i, (a, b) in enumerate(pairs)]
    for copy in copies:
        copy.start()
    for copy in copies[:2]:
        copy.wait()
    for peer in range(SENDERS):
        h = group_of(peer)
        o_ref[peer, :, cols(0)] = k_ref[:, cols(h)]
        o_ref[peer, :, cols(1)] = v_ref[:, cols(h)]
    for copy in copies[2:]:
        copy.wait()
    q = q_ref[...].astype(F32)
    g = g_ref[...].astype(F32)
    zero = jnp.zeros((2, HEAD_DIM), BF16)
    rows = [jnp.concatenate([q[r : r + 1], g[r : r + 1]], axis=0).astype(BF16) for r in range(2)]
    for peer in range(SENDERS):
        h = group_of(peer)
        d = place_of(peer)
        if d < PAIRS:
            pair = rows[d // GROUP][:, cols(h * GROUP + d % GROUP)]
        else:
            pair = zero
        o_ref[peer, :, cols(2)] = pair


def unpack_kernel(x_ref, out_ref, dq_ref, dk_ref, dv_ref):
    peer_at = {(group_of(peer), place_of(peer)): peer for peer in range(SENDERS)}
    for h in range(KV_HEADS):
        total = jnp.zeros((2, 2 * HEAD_DIM), F32)
        for d in range(PEERS):
            total += x_ref[peer_at[h, d], :, : 2 * HEAD_DIM].astype(F32)
        dk_ref[:, cols(h)] = total[:, :HEAD_DIM].astype(BF16)
        dv_ref[:, cols(h)] = total[:, HEAD_DIM:].astype(BF16)
        for n in range(GROUP):
            first = x_ref[peer_at[h, n], :, cols(2)].astype(F32)
            second = x_ref[peer_at[h, GROUP + n], :, cols(2)].astype(F32)
            at = cols(h * GROUP + n)
            out_ref[:, at] = jnp.concatenate([first[:1], second[:1]], axis=0).astype(BF16)
            dq_ref[:, at] = jnp.concatenate([first[1:], second[1:]], axis=0).astype(BF16)


def post_kernel(own_ref, other_ref, pair_ref, o_ref):
    total = (own_ref[...] + other_ref[...].astype(F32)).astype(BF16)
    o_ref[:, :, : 2 * HEAD_DIM] = total.reshape(SENDERS, 2, 2 * HEAD_DIM)
    o_ref[:, :, 2 * HEAD_DIM :] = pair_ref[...].reshape(SENDERS, 2, HEAD_DIM)


def deinterleave(row_axis):
    i = lax.broadcasted_iota(jnp.int32, (HALF, HALF), row_axis)
    j = lax.broadcasted_iota(jnp.int32, (HALF, HALF), 1 - row_axis)
    source = jnp.where(i < SENDERS, 2 * i, 2 * i - HALF + 1)
    return (source == j).astype(BF16)


def seen_by(length):
    u = lax.broadcasted_iota(jnp.int32, (ANS_LEN, ANS_LEN), 0)
    t = lax.broadcasted_iota(jnp.int32, (ANS_LEN, ANS_LEN), 1)
    return (u <= t) & (u < length)


def live_rows(length):
    return lax.broadcasted_iota(jnp.int32, (ANS_LEN, HEAD_DIM), 0) < length


def column_sum(x):
    return jnp.sum(x, axis=0, keepdims=True)


def column_max(x):
    return jnp.max(x, axis=0, keepdims=True)


def own_kernel(
    len_ref, seg_hbm, aq_hbm, ak_hbm, av_hbm, ag_hbm,
    q_ref, g_ref, stat_ref, bias_ref,
    seg_ref, raw_ref, k_ref, v_ref, sems,
):
    pairs = [(seg_hbm, seg_ref), (ak_hbm, k_ref), (av_hbm, v_ref)]
    for n in range(GROUP):
        rows = pl.ds(n * ANS_LEN, ANS_LEN)
        at = pl.ds(n * HEAD_DIM, HEAD_DIM)
        pairs.append((aq_hbm.at[:, at], q_ref.at[rows, :]))
        pairs.append((ag_hbm.at[:, at], raw_ref.at[rows, :]))
    copies = [pltpu.make_async_copy(a, b, sems.at[i]) for i, (a, b) in enumerate(pairs)]
    for copy in copies:
        copy.start()
    length = len_ref[0]
    core = lax.axis_index("c")
    row = jnp.where(lax.axis_index("y") * 4 + lax.axis_index("zh") >= GROUP, 1, 0)

    j = lax.broadcasted_iota(jnp.int32, (PROMPT, 1), 0)
    side = jnp.where(j < HALF, core, 1 - core)
    at = row_at((j & (HALF - 1)) >> 1, side, j & 1)
    key_pick = (at == lax.broadcasted_iota(jnp.int32, (PROMPT, PROMPT), 1)).astype(BF16)
    i = lax.broadcasted_iota(jnp.int32, (SENDERS, 1), 0)
    at = row_at(i, core, row)
    row_pick = (at == lax.broadcasted_iota(jnp.int32, (SENDERS, PROMPT), 1)).astype(BF16)
    copies[0].wait()
    segments = jnp.broadcast_to(seg_ref[...].astype(F32), (SENDERS, PROMPT)).astype(BF16)
    key_segments = dot(key_pick, segments, NT)
    row_segments = dot(segments, row_pick, NT)[:1]
    bias_ref[...] = jnp.where(key_segments <= row_segments, 0.0, NEG)

    seen = seen_by(length)
    live_row = live_rows(length)
    for copy in copies[1:]:
        copy.wait()
    keys = k_ref[...]
    values = v_ref[...]
    for n in range(GROUP):
        grads = raw_ref[head(n)]
        grads = jnp.where(live_row, grads, jnp.zeros_like(grads))
        g_ref[head(n)] = grads
        scores = jnp.where(seen, dot(keys, q_ref[head(n)], NT), NEG)
        top = column_max(scores)
        weights = jnp.exp2(scores * SCALE2 - top * SCALE2)
        stat_ref[0:1, head(n)] = top
        stat_ref[1:2, head(n)] = column_sum(weights)
        stat_ref[2:3, head(n)] = column_sum(weights * dot(values, grads, NT))


def near_kernel(
    bias_ref, own_ref, q_ref, g_ref, stat_ref,
    e_ref, far_bias_ref, stat2_ref, q2_ref, g2_ref,
):
    keys = own_ref[:, cols(0)]
    values = own_ref[:, cols(1)]
    moved = dot(deinterleave(0), own_ref[:, cols(2)], NN).astype(BF16)
    far_bias_ref[...] = bias_ref[HALF:]
    q2_ref[:ROWS] = q_ref[...]
    g2_ref[:ROWS] = g_ref[...]
    q2_ref[ROWS:] = moved[:SENDERS]
    g2_ref[ROWS:] = moved[SENDERS:]
    for n in range(GROUP + 1):
        if n < GROUP:
            scores = dot(keys, q_ref[head(n)], NT)
            prob_grad = dot(values, g_ref[head(n)], NT)
            old_top = stat_ref[0:1, head(n)]
            top = jnp.maximum(column_max(scores), old_top)
        else:
            scores = dot(keys, moved[:SENDERS], NT) + bias_ref[:HALF]
            prob_grad = dot(values, moved[SENDERS:], NT)
            top = column_max(scores)
        weights = jnp.exp2(scores * SCALE2 - top * SCALE2)
        total = column_sum(weights)
        moment = column_sum(weights * prob_grad)
        if n < GROUP:
            shift = jnp.exp2((old_top - top) * SCALE2)
            total += stat_ref[1:2, head(n)] * shift
            moment += stat_ref[2:3, head(n)] * shift
        e_ref[:, head(n)] = weights
        stat2_ref[0:1, head(n)] = top
        stat2_ref[1:2, head(n)] = total
        stat2_ref[2:3, head(n)] = moment


def far_kernel(
    bias_ref, sib_ref, q_ref, g_ref, stat_ref, dsib_ref, w_ref, ds_ref, stat2_ref
):
    scores = dot(sib_ref[:, cols(0)], q_ref[...], NT)
    scores = jnp.concatenate([scores[:, :ROWS], scores[:, ROWS:] + bias_ref[...]], axis=1)
    prob_grad = dot(sib_ref[:, cols(1)], g_ref[...], NT)
    old_top = stat_ref[0:1]
    top = jnp.maximum(column_max(scores), old_top)
    shift = jnp.exp2((old_top - top) * SCALE2)
    weights = jnp.exp2(scores * SCALE2 - top * SCALE2)
    total = column_sum(weights) + stat_ref[1:2] * shift
    moment = column_sum(weights * prob_grad) + stat_ref[2:3] * shift
    inverse = 1.0 / total
    delta = moment * inverse
    stat2_ref[0:1] = top * SCALE2 + jnp.log2(total)
    stat2_ref[1:2] = delta
    stat2_ref[2:3] = shift * inverse
    weights = weights * inverse
    w_ref[...] = weights.astype(BF16)
    ds_ref[...] = (weights * (prob_grad - delta)).astype(BF16)
    dsib_ref[:, cols(0)] = (dot(ds_ref[...], q_ref[...], NN) * SCALING).astype(BF16)
    dsib_ref[:, cols(1)] = dot(w_ref[...], g_ref[...], NN).astype(BF16)


def mine_kernel(
    own_ref, sib_ref, q_ref, g_ref, e_ref, stat_ref, wsib_ref, dssib_ref,
    down_ref, pair_ref, w_ref, ds_ref,
):
    prob_grad = dot(own_ref[:, cols(1)], g_ref[...], NT)
    weights = e_ref[...] * stat_ref[2:3]
    w_ref[...] = weights.astype(BF16)
    ds_ref[...] = (weights * (prob_grad - stat_ref[1:2])).astype(BF16)
    down_ref[:, cols(0)] = dot(ds_ref[...], q_ref[...], NN) * SCALING
    down_ref[:, cols(1)] = dot(w_ref[...], g_ref[...], NN)
    results = []
    for part, near_ref, far_ref, factor in (
        (1, w_ref, wsib_ref, 1.0), (0, ds_ref, dssib_ref, SCALING)
    ):
        turned = dot(own_ref[:, cols(part)].T, near_ref[:, head(GROUP)], NN)
        turned += dot(sib_ref[:, cols(part)].T, far_ref[:, head(GROUP)], NN)
        results.append((turned * factor).T)
    both = jnp.concatenate(results, axis=0).astype(BF16)
    pair_ref[...] = dot(deinterleave(1), both, NN).astype(BF16)


def rest_kernel(
    len_ref, aq_hbm, ak_hbm, av_hbm, ag_hbm, own_ref, sib_ref,
    w_ref, ds_ref, wsib_ref, dssib_ref, stat_ref,
    aout_ref, adq_ref, adk_ref, adv_ref, q_ref, k_ref, v_ref, g_ref, out_ref, dq_ref, sems,
):
    pairs = ((aq_hbm, q_ref), (ak_hbm, k_ref), (av_hbm, v_ref), (ag_hbm, g_ref))
    copies = [pltpu.make_async_copy(a, b, sems.at[i]) for i, (a, b) in enumerate(pairs)]
    for copy in copies:
        copy.start()
    length = len_ref[0]
    seen = seen_by(length)
    live_row = live_rows(length)
    for part, near_ref, far_ref, sum_ref in (
        (1, w_ref, wsib_ref, out_ref), (0, ds_ref, dssib_ref, dq_ref)
    ):
        sum_ref[...] = dot(own_ref[:, cols(part)].T, near_ref[:, :ROWS], NN)
        sum_ref[...] += dot(sib_ref[:, cols(part)].T, far_ref[:, :ROWS], NN)
    for copy in copies:
        copy.wait()
    keys = k_ref[...]
    values = v_ref[...]
    keys_t = keys.T
    values_t = values.T
    dk = jnp.zeros((ANS_LEN, HEAD_DIM), F32)
    dv = jnp.zeros((ANS_LEN, HEAD_DIM), F32)
    for n in range(GROUP):
        queries = q_ref[:, cols(n)]
        grads = g_ref[:, cols(n)]
        grads = jnp.where(live_row, grads, jnp.zeros_like(grads))
        scores = jnp.where(seen, dot(keys, queries, NT), NEG)
        weights = jnp.exp2(scores * SCALE2 - stat_ref[0:1, head(n)])
        weights_low = weights.astype(BF16)
        product = dot(values, grads, NT) - stat_ref[1:2, head(n)]
        score_grad = (weights * product).astype(BF16)
        out_t = out_ref[:, head(n)] + dot(values_t, weights_low, NN)
        dq_t = dq_ref[:, head(n)] + dot(keys_t, score_grad, NN)
        aout_ref[:, cols(n)] = jnp.where(live_row, out_t.T, 0.0).astype(BF16)
        adq_ref[:, cols(n)] = (dq_t * SCALING).T.astype(BF16)
        dk += dot(score_grad, queries, NN)
        dv += dot(weights_low, grads, NN)
    adk_ref[...] = (dk * SCALING).astype(BF16)
    adv_ref[...] = dv.astype(BF16)


def call(kernel, out_shape, specs, scratch=(), flops=0, moved=0, limit=16):
    return pl.pallas_call(
        kernel,
        out_shape=out_shape,
        in_specs=specs,
        out_specs=jax.tree.map(lambda _: VMEM, out_shape),
        scratch_shapes=list(scratch),
        cost_estimate=pl.CostEstimate(flops=flops, bytes_accessed=moved, transcendentals=0),
        compiler_params=pltpu.CompilerParams(vmem_limit_bytes=limit * 1024 * 1024),
    )


def bf16(*shape):
    return jax.ShapeDtypeStruct(shape, BF16)


def vmem(*shape, dtype=BF16):
    return pltpu.VMEM(shape, dtype)


def in_hbm(x):
    return pltpu.with_memory_space_constraint(x, pltpu.HBM)


def in_vmem(x):
    return pltpu.with_memory_space_constraint(x, pltpu.VMEM)


def exchange(x):
    return lax.all_to_all(
        x, SEQ_AXES + HEAD_AXES, split_axis=0, concat_axis=0, tiled=True,
        axis_index_groups=peer_groups(),
    )


def body(
    prompt_q, prompt_k, prompt_v, prompt_grad, segment_ids,
    answer_q, answer_k, answer_v, answer_grad, answer_lengths,
):
    wide = HEADS * HEAD_DIM
    narrow = KV_HEADS * HEAD_DIM
    group = GROUP * HEAD_DIM
    packed = call(
        pack_kernel,
        bf16(SENDERS, 2, 3 * HEAD_DIM),
        [HBM] * 4,
        scratch=[
            pltpu.VMEM((2, wide), BF16), pltpu.VMEM((2, wide), BF16),
            pltpu.VMEM((2, narrow), BF16), pltpu.VMEM((2, narrow), BF16),
            pltpu.SemaphoreType.DMA((4,)),
        ],
        limit=4,
    )(in_hbm(prompt_q), in_hbm(prompt_grad), in_hbm(prompt_k), in_hbm(prompt_v))
    packed, answer_q = lax.optimization_barrier((packed, answer_q))
    own = exchange(packed)
    own = own.reshape(HALF, 3 * HEAD_DIM)

    queries, grads, stat, bias = call(
        own_kernel,
        (
            vmem(ROWS, HEAD_DIM), vmem(ROWS, HEAD_DIM), vmem(8, ROWS, dtype=F32),
            vmem(PROMPT, SENDERS, dtype=F32),
        ),
        [SMEM] + [HBM] * 5,
        scratch=[
            pltpu.VMEM((1, PROMPT), jnp.int32), pltpu.VMEM((ROWS, HEAD_DIM), BF16),
            pltpu.VMEM((ANS_LEN, HEAD_DIM), BF16), pltpu.VMEM((ANS_LEN, HEAD_DIM), BF16),
            pltpu.SemaphoreType.DMA((3 + 2 * GROUP,)),
        ],
        flops=400_000_000, moved=2_000_000,
    )(
        answer_lengths, in_hbm(segment_ids.reshape(1, PROMPT)), in_hbm(answer_q[0]),
        in_hbm(answer_k[0]), in_hbm(answer_v[0]), in_hbm(answer_grad[0]),
    )
    own, stat = lax.optimization_barrier((own, stat))
    sibling = lax.ppermute(own, "c", OTHER_CORE)
    exps, bias, stat, queries, grads = call(
        near_kernel,
        (
            vmem(HALF, ALL, dtype=F32), vmem(HALF, SENDERS, dtype=F32),
            vmem(8, ALL, dtype=F32), vmem(ALL, HEAD_DIM), vmem(ALL, HEAD_DIM),
        ),
        [VMEM] * 5,
        flops=200_000_000, moved=2_000_000,
    )(bias, own, queries, grads, stat)
    d_sib, far_w, far_ds, stat = call(
        far_kernel,
        (
            vmem(HALF, 2 * HEAD_DIM), vmem(HALF, ALL), vmem(HALF, ALL),
            vmem(8, ALL, dtype=F32),
        ),
        [VMEM] * 5,
        flops=400_000_000, moved=2_000_000,
    )(bias, sibling, queries, grads, stat)

    d_mine = lax.ppermute(d_sib, "c", OTHER_CORE)
    d_own, pair, near_w, near_ds = call(
        mine_kernel,
        (
            vmem(HALF, 2 * HEAD_DIM, dtype=F32), vmem(HALF, HEAD_DIM),
            vmem(HALF, ALL), vmem(HALF, ALL),
        ),
        [VMEM] * 8,
        flops=200_000_000, moved=2_000_000,
    )(own, sibling, queries, grads, exps, stat, far_w, far_ds)
    back = call(
        post_kernel, bf16(SENDERS, 2, 3 * HEAD_DIM), [VMEM] * 3, limit=4, moved=700_000
    )(d_own, d_mine, pair)
    back, stat = lax.optimization_barrier((back, stat))
    back = exchange(back)
    a_out, a_dq, a_dk, a_dv = call(
        rest_kernel,
        (
            bf16(ANS_LEN, group), bf16(ANS_LEN, group),
            bf16(ANS_LEN, HEAD_DIM), bf16(ANS_LEN, HEAD_DIM),
        ),
        [SMEM] + [HBM] * 4 + [VMEM] * 7,
        scratch=[
            pltpu.VMEM((ANS_LEN, group), BF16), pltpu.VMEM((ANS_LEN, HEAD_DIM), BF16),
            pltpu.VMEM((ANS_LEN, HEAD_DIM), BF16), pltpu.VMEM((ANS_LEN, group), BF16),
            pltpu.VMEM((HEAD_DIM, ROWS), F32), pltpu.VMEM((HEAD_DIM, ROWS), F32),
            pltpu.SemaphoreType.DMA((4,)),
        ],
        flops=700_000_000, moved=2_000_000,
    )(
        answer_lengths, in_hbm(answer_q[0]), in_hbm(answer_k[0]), in_hbm(answer_v[0]),
        in_hbm(answer_grad[0]), own, sibling, near_w, near_ds, far_w, far_ds, stat,
    )
    p_out, p_dq, p_dk, p_dv = call(
        unpack_kernel, (bf16(2, wide), bf16(2, wide), bf16(2, narrow), bf16(2, narrow)), [VMEM],
        limit=4,
    )(in_vmem(back))
    return (p_out, p_dq, p_dk, p_dv, a_out[None], a_dq[None], a_dk[None], a_dv[None])


def solution(mesh):
    grid = Mesh(mesh.devices.reshape(4, 4, 2, 4, 2), SEQ_AXES + HEAD_AXES)
    rows = P(SEQ_AXES + HEAD_AXES, None)
    answers = P(SEQ_AXES, None, HEAD_AXES)
    return jax.shard_map(
        body,
        mesh=grid,
        in_specs=(rows, rows, rows, rows, P(), answers, answers, answers, answers, P(SEQ_AXES)),
        out_specs=(rows, rows, rows, rows, answers, answers, answers, answers),
        check_vma=False,
    )
```
